128 devices in a mesh: passage: 8 (over x, core), span: 16 (over z, y).
Axes of the slice: x: 4, y: 4, z: 4, core: 2. Of those that a mesh axis runs over, the one named last changes fastest.
Arguments:
- snapshots: bfloat16 [5, 256, 384, 1024], P(None, 'passage', 'span'), may hold values from -23 to 23
- sketch: bfloat16 [1024, 144], replicated, may hold values from -0.1875 to 0.1875
- blade_row: int32 [256], P('passage'), may hold values from 0 to 1
- row_speed: float32 [2], replicated, may hold values from 0.5 to 1.5
- stencil_reach: int32 [384], P('span'), may hold values from 1 to 2, as said below
Outputs:
- basis: float32 [15, 256, 384, 144], P(None, 'passage', 'span')
- coefficients: float32 [1024, 144], P(('passage', 'span'))
The draws below stay inside these ranges and needn't reach their ends.
Inputs may be any that keep to these rules, and one draw needn't show every extreme that they name: `stencil_reach`: both offsets occur.
All inputs are finite; a program needn't handle non-finite values.
Results may differ from the reference program's by a relative error of at most 0.0037.
The reference program's roundings to bfloat16 on the way (of `fields` and `sketched`) count: a program that leaves them out, or rounds other values in their place, can miss the bound.
Values may be sent and summed in bfloat16 or wider, within the bound.
No kernel may reach another device: no remote copies, remote signals or barrier semaphores. Data moves between devices by JAX's collectives and lax.ppermute only.
A program may use at most 192 MiB of HBM per device.

```python
import math
import jax
import jax.numpy as jnp
from jax import lax

VARS = 5
SNAP = 1024
RANK = 144
BROWS = 2
NT = 256
NR = 384


def draw_snapshots(key, part):
    keys = jax.random.split(key, 4)
    shape = (VARS, NT, NR, SNAP)
    low_log = math.log(0.56)
    high_log = math.log(1.78)
    column_scale = jnp.exp(jax.random.uniform(keys[1], (1, NT, 1, 1), jnp.float32, low_log, high_log))
    line_scale = jnp.exp(jax.random.uniform(keys[2], (1, 1, NR, 1), jnp.float32, low_log, high_log))
    moment_scale = jnp.exp(jax.random.uniform(keys[3], (1, 1, 1, SNAP), jnp.float32, low_log, high_log))
    values = jnp.clip(jax.random.normal(keys[0], shape, jnp.float32), -4.0, 4.0)
    return (values * column_scale * line_scale * moment_scale).astype(jnp.bfloat16)


def draw_stencil_reach(key, part):
    first_key, second_key = jax.random.split(key)
    values = jax.random.randint(first_key, (NR,), 1, 3).astype(jnp.int32)
    places = jax.random.permutation(second_key, NR)
    values = values.at[places[0]].set(2)
    values = values.at[places[1]].set(1)
    return values


def set_ends(array, rng, low, high):
    shape = array.shape
    index_at = [jax.random.randint(jax.random.fold_in(rng, axis), (), 0, shape[axis]) for axis in range(len(shape))]
    array = array.at[tuple(index_at)].set(low)
    longest = shape.index(max(shape))
    index_at[longest] = (index_at[longest] + 1) % shape[longest]
    return array.at[tuple(index_at)].set(high)


def scatter_about(own_key, dims, scale, reach, held_as=jnp.bfloat16):
    values = jax.random.normal(own_key, dims, jnp.float32) * scale
    return jnp.minimum(jnp.maximum(values, -reach), reach).astype(held_as)


def setup_inputs(seed: int = 0) -> dict:
    streams_of = jax.random.split(jax.random.key(seed), 6)
    return {
        "snapshots": draw_snapshots(jax.random.fold_in(streams_of[5], 71), 0),
        "sketch": scatter_about(streams_of[1], (SNAP, RANK), SNAP ** -0.5, 0.1875),
        "blade_row": set_ends(jax.random.randint(streams_of[2], (NT,), 0, BROWS), jax.random.fold_in(streams_of[2], 1), 0, BROWS - 1).astype(jnp.int32),
        "row_speed": jnp.clip(jax.random.uniform(streams_of[3], (BROWS,), jnp.float32, 0.5, 1.5), 0.5, 1.5),
        "stencil_reach": draw_stencil_reach(jax.random.fold_in(streams_of[5], 71), 0),
    }


def frame_of(blade_row, row_speed, radial_pos, radial_total):
    radius = 0.6 + 0.4 * (radial_pos + 0.5) / radial_total
    labels = jnp.arange(row_speed.shape[0], dtype=jnp.int32)
    column_speed = lax.optimization_barrier(jnp.sum(jnp.where(blade_row[:, None] == labels[None, :], row_speed[None, :], 0.0), axis=1))
    return column_speed[:, None] * radius[None, :]

def transform(snapshots, frame_shift):
    density = snapshots[0].astype(jnp.float32)
    axial_vel = snapshots[1].astype(jnp.float32)
    swirl_vel = snapshots[2].astype(jnp.float32) + frame_shift[:, :, None]
    radial_vel = snapshots[3].astype(jnp.float32)
    kinetic = axial_vel * axial_vel + swirl_vel * swirl_vel + radial_vel * radial_vel
    total_press = snapshots[4].astype(jnp.float32) + 0.05 * (1.0 + 0.2 * jnp.tanh(density)) * kinetic
    return jnp.stack([density, axial_vel, swirl_vel, radial_vel, total_press]).astype(jnp.bfloat16)

def inverse_t(gram_total):
    factor = jnp.linalg.cholesky(gram_total)
    unit_matrix = jnp.eye(gram_total.shape[0], dtype=gram_total.dtype)
    lower_inv = lax.linalg.triangular_solve(factor, unit_matrix, left_side=True, lower=True)
    return lower_inv.T

def reference(snapshots, sketch, blade_row, row_speed, stencil_reach):
    variables, theta_total, radial_total, columns = snapshots.shape
    sketch_width = sketch.shape[1]
    radial_pos = jnp.arange(radial_total).astype(jnp.float32)
    frame_shift = frame_of(blade_row, row_speed, radial_pos, radial_total)
    fields = transform(snapshots, frame_shift)
    row_total = 3 * variables * theta_total * radial_total
    families = [[], [], []]
    gram_total = jnp.zeros((sketch_width, sketch_width), jnp.float32)
    projected = jnp.zeros((columns, sketch_width), jnp.float32)
    wide_line = (stencil_reach == 2)[None, :, None]
    sketch_wide = sketch.astype(jnp.float32)
    for variable in range(variables):
        one_field = fields[variable].astype(jnp.float32)
        nearer = 0.5 * (jnp.roll(one_field, -1, axis=0) - jnp.roll(one_field, 1, axis=0))
        farther = 0.25 * (jnp.roll(one_field, -2, axis=0) - jnp.roll(one_field, 2, axis=0))
        turning = jnp.where(wide_line, farther, nearer)
        radial_pad = jnp.pad(one_field, ((0, 0), (1, 1), (0, 0)))
        spanwise = 0.5 * (radial_pad[:, 2:] - radial_pad[:, :-2])
        for family_index, member in enumerate((one_field, turning, spanwise)):
            matrix = member.reshape(theta_total * radial_total, columns)
            sketched = jnp.dot(matrix, sketch_wide, precision=lax.Precision.HIGHEST).astype(jnp.bfloat16)
            gram_total = gram_total + jnp.dot(sketched.T.astype(jnp.float32), sketched.astype(jnp.float32), preferred_element_type=jnp.float32)
            projected = projected + jnp.dot(matrix.T, sketched.astype(jnp.float32), precision=lax.Precision.HIGHEST)
            families[family_index].append(sketched)
    inv_factor = inverse_t(gram_total)
    row_scale = math.sqrt(row_total)
    basis_list = []
    for family in families:
        for sketched in family:
            product = jnp.dot(sketched.astype(jnp.float32), inv_factor, precision=lax.Precision.HIGHEST)
            basis_list.append((product * row_scale).reshape(theta_total, radial_total, sketch_width))
    basis = jnp.stack(basis_list)
    coefficients = jnp.dot(projected, inv_factor, precision=lax.Precision.HIGHEST) / row_scale
    return (basis, coefficients)
```

```python
import functools
import math

import jax
import jax.numpy as jnp
from jax import lax
from jax.experimental import pallas as pl
from jax.experimental.pallas import tpu as pltpu
from jax.sharding import PartitionSpec as P

F32 = jnp.float32
BF16 = jnp.bfloat16
MIB = 1024 * 1024


def params(mib, **kw):
    return pltpu.CompilerParams(vmem_limit_bytes=mib * MIB, **kw)


def fields_kernel(radial_total, lines, blade_ref, speed_ref, snap_ref, sketch_ref,
                  field_ref, y_ref, first_t_ref, last_t_ref, first_r_ref, last_r_ref):
    step = pl.program_id(0)
    steps = pl.num_programs(0)
    variables, rows, columns = snap_ref.shape
    group = 2 * lines
    cells = rows // lines
    row_id = lax.broadcasted_iota(jnp.int32, (group, 128), 0)
    line_id = jnp.where(row_id >= lines, row_id - lines, row_id)
    radial_pos = (lax.axis_index("span") * lines + line_id).astype(F32)
    radius = 0.6 + 0.4 * (radial_pos + 0.5) / radial_total

    def column_speed(cell):
        label = blade_ref[step * cells + cell]
        total = jnp.float32(0.0)
        for row in range(speed_ref.shape[0]):
            total = jnp.where(label == row, speed_ref[row], total)
        return total

    for pair in range(rows // group):
        speed = jnp.where(row_id < lines, column_speed(2 * pair), column_speed(2 * pair + 1))
        shift = speed * radius
        at = pl.ds(pair * group, group)
        for tile in range(columns // 128):
            lanes = pl.ds(tile * 128, 128)
            density = snap_ref[0, at, lanes].astype(F32)
            axial = snap_ref[1, at, lanes].astype(F32)
            swirl = snap_ref[2, at, lanes].astype(F32) + shift
            radial = snap_ref[3, at, lanes].astype(F32)
            kinetic = axial * axial + swirl * swirl + radial * radial
            press = snap_ref[4, at, lanes].astype(F32) + 0.05 * (1.0 + 0.2 * jnp.tanh(density)) * kinetic
            field_ref[0, at, lanes] = snap_ref[0, at, lanes]
            field_ref[1, at, lanes] = snap_ref[1, at, lanes]
            field_ref[2, at, lanes] = swirl.astype(BF16)
            field_ref[3, at, lanes] = snap_ref[3, at, lanes]
            field_ref[4, at, lanes] = press.astype(BF16)
    for v in range(variables):
        y_ref[v] = lax.dot_general(field_ref[v], sketch_ref[...], (((1,), (1,)), ((), ())),
                                   preferred_element_type=F32)
        for cell in range(cells):
            for side in range(2):
                row = cell * lines + side
                first_r_ref[side, v, cell:cell + 1] = y_ref[v, row:row + 1]
                row = row + lines - 2
                last_r_ref[side, v, cell:cell + 1] = y_ref[v, row:row + 1]

    edge = first_t_ref.shape[1]

    @pl.when(step == 0)
    def _():
        first_t_ref[...] = y_ref[:, :edge, :]

    @pl.when(step == steps - 1)
    def _():
        last_t_ref[...] = y_ref[:, rows - edge:, :]


def fields_and_sketch(snapshots, sketch_t, blade_row, row_speed, lines, radial_total):
    variables, rows, columns = snapshots.shape
    width = sketch_t.shape[0]
    steps = 4
    block = rows // steps
    cells = rows // lines
    edge = 4 * lines
    return pl.pallas_call(
        functools.partial(fields_kernel, radial_total, lines),
        grid=(steps,),
        in_specs=[
            pl.BlockSpec(memory_space=pltpu.SMEM),
            pl.BlockSpec(memory_space=pltpu.SMEM),
            pl.BlockSpec((variables, block, columns), lambda i: (0, i, 0)),
            pl.BlockSpec((width, columns), lambda i: (0, 0)),
        ],
        out_specs=[
            pl.BlockSpec((variables, block, columns), lambda i: (0, i, 0)),
            pl.BlockSpec((variables, block, width), lambda i: (0, i, 0)),
            pl.BlockSpec((variables, edge, width), lambda i: (0, 0, 0)),
            pl.BlockSpec((variables, edge, width), lambda i: (0, 0, 0)),
            pl.BlockSpec((2, variables, cells // steps, width), lambda i: (0, 0, i, 0)),
            pl.BlockSpec((2, variables, cells // steps, width), lambda i: (0, 0, i, 0)),
        ],
        out_shape=[
            jax.ShapeDtypeStruct((variables, rows, columns), BF16),
            jax.ShapeDtypeStruct((variables, rows, width), F32),
            jax.ShapeDtypeStruct((variables, edge, width), F32),
            jax.ShapeDtypeStruct((variables, edge, width), F32),
            jax.ShapeDtypeStruct((2, variables, cells, width), F32),
            jax.ShapeDtypeStruct((2, variables, cells, width), F32),
        ],
        compiler_params=params(40),
        name="fields_sketch",
    )(blade_row, row_speed, snapshots, sketch_t)


def stencil_kernel(lines, reach_ref, y_ref, before_t_ref, after_t_ref, before_r_ref, after_r_ref,
                   z_ref, w_ref, gram_ref, acc_ref):
    v = pl.program_id(0)
    rows, width = y_ref.shape[1:]
    cells = rows // lines
    wide = reach_ref[...] == 2
    scale = jnp.where(wide, 0.25, 0.5)
    row_id = lax.broadcasted_iota(jnp.int32, (lines, width), 0)
    span = lax.axis_index("span")
    has_before = jnp.where(span > 0, 0.5, 0.0).astype(F32)
    has_after = jnp.where(span < lax.axis_size("span") - 1, 0.5, 0.0).astype(F32)

    def y_at(t):
        if t < 0:
            return before_t_ref[0, (t + 4) * lines:(t + 5) * lines, :]
        if t >= cells:
            return after_t_ref[0, (t - cells) * lines:(t - cells + 1) * lines, :]
        return y_ref[0, t * lines:(t + 1) * lines, :]

    def turn(get, t):
        return scale * jnp.where(wide, get(t + 2) - get(t - 2), get(t + 1) - get(t - 1))

    def rounded(x):
        return x.astype(BF16).astype(F32)

    z1 = {}

    def z1_at(t):
        if t not in z1:
            z1[t] = rounded(turn(y_at, t))
        return z1[t]

    def down(x, end):
        return jnp.where(row_id == 0, end, pltpu.roll(x, 1, 0))

    def up(x, end):
        return jnp.where(row_id == lines - 1, end, pltpu.roll(x, lines - 1, 0))

    for pair in range(cells // 2):
        kept = []
        for t in (2 * pair, 2 * pair + 1):
            y = y_at(t)
            w1 = -turn(z1_at, t)
            one = slice(t, t + 1)
            before2, before1 = before_r_ref[0, 0, one, :], before_r_ref[1, 0, one, :]
            after1, after2 = after_r_ref[0, 0, one, :], after_r_ref[1, 0, one, :]
            z2 = rounded(0.5 * (up(y, after1) - down(y, before1)))
            z2_before = rounded(has_before * (y[0:1] - before2))
            z2_after = rounded(has_after * (after2 - y[lines - 1:lines]))
            w2 = 0.5 * (down(z2, z2_before) - up(z2, z2_after))
            kept.append((y, z1_at(t), z2, rounded(y) + w1 + w2))
        at = pl.ds(2 * pair * lines, 2 * lines)
        a, b = kept
        for family in range(3):
            z_ref[family, 0, at, :] = jnp.concatenate([a[family], b[family]], axis=0).astype(BF16)
        w_ref[0, at, :] = jnp.concatenate([a[3], b[3]], axis=0).astype(BF16)

    gram = jnp.zeros((width, width), F32)
    for family in range(3):
        z = z_ref[family, 0]
        gram = gram + lax.dot_general(z, z, (((0,), (0,)), ((), ())), preferred_element_type=F32)

    @pl.when(v == 0)
    def _():
        acc_ref[...] = gram

    @pl.when(v > 0)
    def _():
        acc_ref[...] += gram

    @pl.when(v == pl.num_programs(0) - 1)
    def _():
        gram_ref[:width, :] = acc_ref[:, :128]
        gram_ref[width:, :] = jnp.zeros((gram_ref.shape[0] - width, 128), F32)
        gram_ref[width:, :width - 128] = acc_ref[128:, 128:]


def stencils(y, before_t, after_t, before_r, after_r, reach, lines):
    variables, rows, width = y.shape
    cells = rows // lines
    edge = 4 * lines
    packed = width + (width - 128)
    return pl.pallas_call(
        functools.partial(stencil_kernel, lines),
        grid=(variables,),
        in_specs=[
            pl.BlockSpec((lines, width), lambda v: (0, 0)),
            pl.BlockSpec((1, rows, width), lambda v: (v, 0, 0)),
            pl.BlockSpec((1, edge, width), lambda v: (v, 0, 0)),
            pl.BlockSpec((1, edge, width), lambda v: (v, 0, 0)),
            pl.BlockSpec((2, 1, cells, width), lambda v: (0, v, 0, 0)),
            pl.BlockSpec((2, 1, cells, width), lambda v: (0, v, 0, 0)),
        ],
        out_specs=[
            pl.BlockSpec((3, 1, rows, width), lambda v: (0, v, 0, 0)),
            pl.BlockSpec((1, rows, width), lambda v: (v, 0, 0)),
            pl.BlockSpec((packed, 128), lambda v: (0, 0)),
        ],
        out_shape=[
            jax.ShapeDtypeStruct((3, variables, rows, width), BF16),
            jax.ShapeDtypeStruct((variables, rows, width), BF16),
            jax.ShapeDtypeStruct((packed, 128), F32),
        ],
        scratch_shapes=[pltpu.VMEM((width, width), F32)],
        compiler_params=params(40),
        name="stencils",
    )(reach, y, before_t, after_t, before_r, after_r)


def project_kernel(field_ref, w_ref, out_ref, acc_ref):
    v = pl.program_id(0)
    part = lax.dot_general(w_ref[0], field_ref[0], (((0,), (0,)), ((), ())), preferred_element_type=F32)

    @pl.when(v == 0)
    def _():
        acc_ref[...] = part

    @pl.when(v > 0)
    def _():
        acc_ref[...] += part

    @pl.when(v == pl.num_programs(0) - 1)
    def _():
        out_ref[...] = acc_ref[...].T.astype(out_ref.dtype)


def project(fields, w):
    variables, rows, columns = fields.shape
    width = w.shape[2]
    return pl.pallas_call(
        project_kernel,
        grid=(variables,),
        in_specs=[
            pl.BlockSpec((1, rows, columns), lambda v: (v, 0, 0)),
            pl.BlockSpec((1, rows, width), lambda v: (v, 0, 0)),
        ],
        out_specs=pl.BlockSpec((columns, width), lambda v: (0, 0)),
        out_shape=jax.ShapeDtypeStruct((columns, width), F32),
        scratch_shapes=[pltpu.VMEM((width, columns), F32)],
        compiler_params=params(40),
        cost_estimate=pl.CostEstimate(flops=2 * variables * rows * columns * 256,
                                      bytes_accessed=variables * rows * columns * 2, transcendentals=0),
        name="project",
    )(fields, w)


def split3(x):
    high = x.astype(BF16)
    rest = x - high.astype(F32)
    mid = rest.astype(BF16)
    return high, mid, (rest - mid.astype(F32)).astype(BF16)


def inverse_factor_kernel(width, gram_ref, out_ref, a_ref):
    size = 16
    packed = gram_ref[...]
    a_ref[...] = jnp.zeros_like(a_ref)
    a_ref[:, :128] = packed[:width]
    a_ref[:128, 128:width] = packed[128:width].T
    a_ref[128:, 128:width] = packed[width:, :width - 128]
    a_ref[:, 256:] = jnp.where(
        lax.broadcasted_iota(jnp.int32, (width, 256), 0) == lax.broadcasted_iota(jnp.int32, (width, 256), 1),
        1.0, 0.0)
    row = lax.broadcasted_iota(jnp.int32, (size, 128), 0)
    lane = lax.broadcasted_iota(jnp.int32, (size, 256), 1)
    for start in range(0, width, size):
        panels = [a_ref[start:start + size, tile * 128:(tile + 1) * 128] for tile in range(4)]
        tile, offset = start // 128, start % 128
        cols = [jnp.broadcast_to(panels[tile][:, offset + j:offset + j + 1], (size, 128)) for j in range(size)]
        for j in range(size):
            pivot = jnp.broadcast_to(cols[j][j:j + 1, :], (size, 128))
            inv = lax.rsqrt(pivot)
            inv = inv * (1.5 - 0.5 * pivot * inv * inv)
            low = cols[j] * inv
            for i in range(j + 1, size):
                cols[i] = cols[i] - low * jnp.broadcast_to(low[i:i + 1, :], (size, 128))
            below = jnp.where(row > j, low, 0.0)
            for p in range(4):
                lead = jnp.broadcast_to(panels[p][j:j + 1, :], (size, 128)) * inv
                panels[p] = jnp.where(row == j, lead, panels[p] - below * lead)
        out_ref[start:start + size, :] = jnp.concatenate([panels[2], panels[3]], axis=1)[:, :width]
        if start + size < width:
            whole = jnp.concatenate(panels, axis=1)
            left = jnp.where(lane >= start + size, whole[:, :256], 0.0)
            lh, lm, ll = split3(left)
            rh, rm, rl = split3(whole)
            lhs = jnp.concatenate([lh, lh, lm, lm, lh, ll], axis=0)
            rhs = jnp.concatenate([rh, rm, rh, rm, rl, rh], axis=0)
            update = lax.dot_general(lhs, rhs, (((0,), (0,)), ((), ())), preferred_element_type=F32)
            a_ref[start + size:, :] -= update[start + size:width, :]


def inverse_factor(gram, width):
    return pl.pallas_call(
        functools.partial(inverse_factor_kernel, width),
        in_specs=[pl.BlockSpec(memory_space=pltpu.VMEM)],
        out_specs=pl.BlockSpec(memory_space=pltpu.VMEM),
        out_shape=jax.ShapeDtypeStruct((width, width), F32),
        scratch_shapes=[pltpu.VMEM((width, 512), F32)],
        compiler_params=params(32),
        name="inverse_factor",
    )(gram)


def basis_kernel(scale, z_ref, inv_ref, out_ref):
    inv = inv_ref[...] * scale
    high = inv.astype(BF16)
    low = (inv - high.astype(F32)).astype(BF16)
    nt = (((1,), (1,)), ((), ()))
    z = z_ref[...]
    out_ref[...] = (lax.dot_general(z, low, nt, preferred_element_type=F32)
                    + lax.dot_general(z, high, nt, preferred_element_type=F32))


def basis_of(z, inv, scale):
    rows, width = z.shape
    block = rows // 10
    return pl.pallas_call(
        functools.partial(basis_kernel, scale),
        grid=(rows // block,),
        in_specs=[
            pl.BlockSpec((block, width), lambda i: (i, 0)),
            pl.BlockSpec((width, width), lambda i: (0, 0)),
        ],
        out_specs=pl.BlockSpec((block, width), lambda i: (i, 0)),
        out_shape=jax.ShapeDtypeStruct((rows, width), F32),
        compiler_params=params(32),
        cost_estimate=pl.CostEstimate(flops=4 * rows * 256 * 256, bytes_accessed=rows * 256 * 6, transcendentals=0),
        name="basis",
    )(z, inv)


def coefficients_kernel(scale, parts_ref, inv_ref, out_ref):
    owned = jnp.sum(parts_ref[...].astype(F32), axis=0)
    out_ref[...] = lax.dot_general(owned, inv_ref[...], (((1,), (1,)), ((), ())),
                                   precision=lax.Precision.HIGHEST, preferred_element_type=F32) * scale


def coefficients_of(parts, inv, scale):
    _, rows, width = parts.shape
    return pl.pallas_call(
        functools.partial(coefficients_kernel, scale),
        in_specs=[pl.BlockSpec(memory_space=pltpu.VMEM)] * 2,
        out_specs=pl.BlockSpec(memory_space=pltpu.VMEM),
        out_shape=jax.ShapeDtypeStruct((rows, width), F32),
        compiler_params=params(32),
        name="coefficients",
    )(parts, inv)


def reduce_all(x):
    passages, layers = lax.axis_size("passage"), lax.axis_size("span")

    def exchange(x, axis, length, moves):
        parts = [lax.ppermute(x, axis, [(i, move(i)) for i in range(length)]) for move in moves]
        for part in parts:
            x = x + part
        return x

    x = exchange(x, "passage", passages, [lambda i: i ^ 1])
    x = exchange(x, "passage", passages, [lambda i, k=k: (i + 2 * k) % passages for k in (2, 1, 3)])
    x = exchange(x, "span", layers, [lambda i, k=k: i // 4 * 4 + (i + k) % 4 for k in (2, 1, 3)])
    x = exchange(x, "span", layers, [lambda i, k=k: (i + 4 * k) % layers for k in (2, 1, 3)])
    return x


def shards(snapshots, sketch, blade_row, row_speed, stencil_reach):
    variables, cells, lines, columns = snapshots.shape
    width = sketch.shape[1]
    passages, layers = lax.axis_size("passage"), lax.axis_size("span")
    row_total = 3 * variables * cells * passages * lines * layers
    fields, y, first_t, last_t, first_r, last_r = fields_and_sketch(
        snapshots.reshape(variables, cells * lines, columns), sketch.T, blade_row, row_speed,
        lines, lines * layers)
    ring_up = [(i, (i + 1) % passages) for i in range(passages)]
    ring_down = [(j, i) for i, j in ring_up]
    line_up = [(i, i + 1) for i in range(layers - 1)]
    line_down = [(j, i) for i, j in line_up]
    before_t = lax.ppermute(last_t, "passage", ring_up)
    after_t = lax.ppermute(first_t, "passage", ring_down)
    before_r = lax.ppermute(last_r, "span", line_up)
    after_r = lax.ppermute(first_r, "span", line_down)
    reach = jnp.broadcast_to(stencil_reach[:, None], (lines, width))
    z, w, gram = stencils(y, before_t, after_t, before_r, after_r, reach, lines)
    projected = project(fields, w)
    gram = reduce_all(gram)
    owned = columns // (passages * layers)
    parts = lax.all_to_all(projected.reshape(passages * layers, owned, width), ("passage", "span"), 0, 0, tiled=True)
    inv = inverse_factor(gram, width)
    basis = basis_of(z.reshape(-1, width), inv, math.sqrt(row_total))
    coefficients = coefficients_of(parts, inv, 1.0 / math.sqrt(row_total))
    return basis.reshape(3 * variables, cells, lines, width), coefficients


def solution(mesh):
    return jax.shard_map(
        shards,
        mesh=mesh,
        in_specs=(P(None, "passage", "span", None), P(), P("passage"), P(), P("span")),
        out_specs=(P(None, "passage", "span", None), P(("passage", "span"), None)),
        check_vma=False,
    )
```

```python
import functools
import math

import jax
import jax.numpy as jnp
from jax import lax
from jax.experimental import pallas as pl
from jax.experimental.pallas import tpu as pltpu
from jax.sharding import PartitionSpec as P

F32 = jnp.float32
BF16 = jnp.bfloat16
MIB = 1024 * 1024
K1_MIB = 24
K1_CHUNKS = 8
K4_BLOCKS = 10
K2_MIB = 24
K3_MIB = 24
K4_MIB = 24


def in_hbm(x):
    return pltpu.with_memory_space_constraint(x, pltpu.HBM)


def params(mib, **kw):
    return pltpu.CompilerParams(vmem_limit_bytes=mib * MIB, **kw)


def packed_rows(rows, groups):
    return rows + rows // groups


def pack(dst_ref, v, value, groups):
    rows, width = value.shape
    part = rows // groups
    rest = value[:, 128:]
    tail = [rest[g * part:(g + 1) * part] for g in range(groups)]
    spare = 128 - groups * (width - 128)
    if spare:
        tail.append(jnp.zeros((part, spare), value.dtype))
    dst_ref[v, :rows] = value[:, :128].astype(BF16)
    dst_ref[v, rows:] = jnp.concatenate(tail, axis=1).astype(BF16)


def unpack(dst_ref, src_ref, v, groups):
    rows, width = dst_ref.shape
    part = rows // groups
    extra = width - 128
    dst_ref[:, :128] = src_ref[v, :rows].astype(F32)
    rest = src_ref[v, rows:].astype(F32)
    for g in range(groups):
        dst_ref[g * part:(g + 1) * part, 128:] = rest[:, g * extra:(g + 1) * extra]


T_GROUPS = 6
R_GROUPS = 4
VMEM_SPEC = pl.BlockSpec(memory_space=pltpu.VMEM)
HBM_SPEC = pl.BlockSpec(memory_space=pltpu.HBM)


def fields_kernel(radial_total, lines, blade_hbm, speed_hbm, sketch_hbm, snap_hbm,
                  field_ref, y_ref, first_t_ref, last_t_ref, first_r_ref, last_r_ref,
                  blade_ref, speed_ref, sketch_ref, turned_ref, low_r_ref, high_r_ref, small_sems, sems):
    variables, rows, columns = field_ref.shape
    chunks = sems.shape[0]
    part = rows // chunks
    group = 2 * lines
    cells = part // lines
    spare = rows // lines
    small = [pltpu.make_async_copy(blade_hbm, blade_ref, small_sems.at[0]),
             pltpu.make_async_copy(speed_hbm, speed_ref, small_sems.at[1]),
             pltpu.make_async_copy(sketch_hbm, sketch_ref, small_sems.at[2])]
    for copy in small:
        copy.start()

    def copy_of(c):
        at = pl.ds(pl.multiple_of(c * part, part), part)
        return pltpu.make_async_copy(snap_hbm.at[:, at], field_ref.at[:, at], sems.at[c])

    for c in range(chunks):
        copy_of(c).start()
    row_id = lax.broadcasted_iota(jnp.int32, (group, 128), 0)
    line_id = jnp.where(row_id >= lines, row_id - lines, row_id)
    radial_pos = (lax.axis_index("span") * lines + line_id).astype(F32)
    radius = 0.6 + 0.4 * (radial_pos + 0.5) / radial_total
    for copy in small:
        copy.wait()
    turned_ref[...] = sketch_ref[...].T

    def column_speed(cell):
        label = blade_ref[cell]
        total = jnp.float32(0.0)
        for row in range(speed_ref.shape[0]):
            total = jnp.where(label == row, speed_ref[row], total)
        return total

    def one_chunk(c, carry):
        copy_of(c).wait()
        base = pl.multiple_of(c * part, part)
        def one_pair(pair, carry):
            cell = c * cells + 2 * pair
            speed = jnp.where(row_id < lines, column_speed(cell), column_speed(cell + 1))
            shift = speed * radius
            at = pl.ds(pl.multiple_of(base + pair * group, group), group)
            for tile in range(columns // 128):
                lanes = pl.ds(tile * 128, 128)
                density = field_ref[0, at, lanes].astype(F32)
                axial = field_ref[1, at, lanes].astype(F32)
                swirl = field_ref[2, at, lanes].astype(F32) + shift
                radial = field_ref[3, at, lanes].astype(F32)
                kinetic = axial * axial + swirl * swirl + radial * radial
                press = (field_ref[4, at, lanes].astype(F32)
                         + 0.05 * (1.0 + 0.2 * jnp.tanh(density)) * kinetic)
                field_ref[2, at, lanes] = swirl.astype(BF16)
                field_ref[4, at, lanes] = press.astype(BF16)
            return carry

        lax.fori_loop(0, part // group, one_pair, 0)
        block = pl.ds(base, part)
        y = jnp.dot(field_ref[:, block].reshape(variables * part, columns), turned_ref[...],
                    preferred_element_type=F32)
        for v in range(variables):
            y_ref[v, block] = y[v * part:(v + 1) * part]
            for cell in range(cells):
                for side in range(2):
                    to = pl.ds(side * spare + c * cells + cell, 1)
                    row = v * part + cell * lines + side
                    low_r_ref[v, to] = y[row:row + 1]
                    row = row + lines - 2
                    high_r_ref[v, to] = y[row:row + 1]
        return carry

    lax.fori_loop(0, chunks, one_chunk, 0)
    for v in range(variables):
        pack(first_t_ref, v, y_ref[v, :4 * lines], T_GROUPS)
        pack(last_t_ref, v, y_ref[v, rows - 4 * lines:], T_GROUPS)
        pack(first_r_ref, v, low_r_ref[v], R_GROUPS)
        pack(last_r_ref, v, high_r_ref[v], R_GROUPS)


def fields_and_sketch(snapshots, sketch_t, blade_row, row_speed, lines, radial_total):
    variables, rows, columns = snapshots.shape
    width = sketch_t.shape[0]
    chunks = K1_CHUNKS
    cells = rows // lines
    edge_t = jax.ShapeDtypeStruct((variables, packed_rows(4 * lines, T_GROUPS), 128), BF16)
    edge_r = jax.ShapeDtypeStruct((variables, packed_rows(2 * cells, R_GROUPS), 128), BF16)
    return pl.pallas_call(
        functools.partial(fields_kernel, radial_total, lines),
        in_specs=[HBM_SPEC] * 4,
        out_specs=[VMEM_SPEC] * 6,
        out_shape=[
            jax.ShapeDtypeStruct((variables, rows, columns), BF16),
            jax.ShapeDtypeStruct((variables, rows, width), F32),
            edge_t, edge_t, edge_r, edge_r,
        ],
        scratch_shapes=[
            pltpu.SMEM(blade_row.shape, blade_row.dtype),
            pltpu.SMEM(row_speed.shape, row_speed.dtype),
            pltpu.VMEM(sketch_t.shape, sketch_t.dtype),
            pltpu.VMEM(sketch_t.shape[::-1], sketch_t.dtype),
            pltpu.VMEM((variables, 2 * cells, width), F32),
            pltpu.VMEM((variables, 2 * cells, width), F32),
            pltpu.SemaphoreType.DMA((3,)),
            pltpu.SemaphoreType.DMA((chunks,)),
        ],
        compiler_params=params(K1_MIB),
        name="fields_sketch",
    )(in_hbm(blade_row), in_hbm(row_speed), in_hbm(sketch_t), in_hbm(snapshots))


def stencil_kernel(lines, reach_ref, y_ref, before_t_in, after_t_in, before_r_in, after_r_in,
                   z_out, w_ref, gram_ref, acc_ref, before_t_ref, after_t_ref, before_r_ref, after_r_ref,
                   z_ref, sems):
    variables, rows, width = y_ref.shape
    cells = rows // lines
    wide = reach_ref[...] == 2
    scale = jnp.where(wide, 0.25, 0.5)
    row_id = lax.broadcasted_iota(jnp.int32, (lines, width), 0)
    span = lax.axis_index("span")
    has_before = jnp.where(span > 0, 0.5, 0.0).astype(F32)
    has_after = jnp.where(span < lax.axis_size("span") - 1, 0.5, 0.0).astype(F32)

    def rounded(x):
        return x.astype(BF16).astype(F32)

    def down(x, end):
        return jnp.where(row_id == 0, end, pltpu.roll(x, 1, 0))

    def up(x, end):
        return jnp.where(row_id == lines - 1, end, pltpu.roll(x, lines - 1, 0))

    def copy_of(v):
        return pltpu.make_async_copy(z_ref.at[:, v], z_out.at[:, v], sems.at[v])

    acc_ref[...] = jnp.zeros_like(acc_ref)

    def one_variable(v, carry):
        unpack(before_t_ref, before_t_in, v, T_GROUPS)
        unpack(after_t_ref, after_t_in, v, T_GROUPS)
        unpack(before_r_ref, before_r_in, v, R_GROUPS)
        unpack(after_r_ref, after_r_in, v, R_GROUPS)

        def y_at(t):
            if t < 0:
                return before_t_ref[(t + 4) * lines:(t + 5) * lines, :]
            if t >= cells:
                return after_t_ref[(t - cells) * lines:(t - cells + 1) * lines, :]
            return y_ref[v, t * lines:(t + 1) * lines, :]

        def turn(get, t):
            return scale * jnp.where(wide, get(t + 2) - get(t - 2), get(t + 1) - get(t - 1))

        z1 = {}

        def z1_at(t):
            if t not in z1:
                z1[t] = rounded(turn(y_at, t))
            return z1[t]

        for pair in range(cells // 2):
            kept = []
            for t in (2 * pair, 2 * pair + 1):
                y = y_at(t)
                w1 = -turn(z1_at, t)
                one, two = slice(t, t + 1), slice(cells + t, cells + t + 1)
                before2, before1 = before_r_ref[one, :], before_r_ref[two, :]
                after1, after2 = after_r_ref[one, :], after_r_ref[two, :]
                z2 = rounded(0.5 * (up(y, after1) - down(y, before1)))
                z2_before = rounded(has_before * (y[0:1] - before2))
                z2_after = rounded(has_after * (after2 - y[lines - 1:lines]))
                w2 = 0.5 * (down(z2, z2_before) - up(z2, z2_after))
                kept.append((y, z1_at(t), z2, rounded(y) + w1 + w2))
            at = pl.ds(2 * pair * lines, 2 * lines)
            a, b = kept
            for family in range(3):
                z_ref[family, v, at, :] = jnp.concatenate([a[family], b[family]], axis=0).astype(BF16)
            w_ref[v, at, :] = jnp.concatenate([a[3], b[3]], axis=0).astype(BF16)
        for family in range(3):
            z = z_ref[family, v]
            acc_ref[...] += lax.dot_general(z, z, (((0,), (0,)), ((), ())), preferred_element_type=F32)
        copy_of(v).start()
        return carry

    lax.fori_loop(0, variables, one_variable, 0)
    gram_ref[:width, :] = acc_ref[:, :128]
    gram_ref[width:, :] = jnp.zeros((gram_ref.shape[0] - width, 128), F32)
    gram_ref[width:, :width - 128] = acc_ref[128:, 128:]
    for v in range(variables):
        copy_of(v).wait()


def stencils(y, before_t, after_t, before_r, after_r, reach, lines):
    variables, rows, width = y.shape
    cells = rows // lines
    return pl.pallas_call(
        functools.partial(stencil_kernel, lines),
        in_specs=[VMEM_SPEC] * 6,
        out_specs=[HBM_SPEC, VMEM_SPEC, VMEM_SPEC],
        out_shape=[
            pltpu.HBM((3, variables, rows, width), BF16),
            jax.ShapeDtypeStruct((variables, rows, width), BF16),
            jax.ShapeDtypeStruct((width + (width - 128), 128), F32),
        ],
        scratch_shapes=[
            pltpu.VMEM((width, width), F32),
            pltpu.VMEM((4 * lines, width), F32),
            pltpu.VMEM((4 * lines, width), F32),
            pltpu.VMEM((2 * cells, width), F32),
            pltpu.VMEM((2 * cells, width), F32),
            pltpu.VMEM((3, variables, rows, width), BF16),
            pltpu.SemaphoreType.DMA((variables,)),
        ],
        compiler_params=params(K2_MIB),
        name="stencils",
    )(reach, y, before_t, after_t, before_r, after_r)


def project_kernel(field_ref, w_ref, out_ref, acc_ref):
    for v in range(field_ref.shape[0]):
        part = lax.dot_general(w_ref[v], field_ref[v], (((0,), (0,)), ((), ())), preferred_element_type=F32)
        acc_ref[...] = part if v == 0 else acc_ref[...] + part
    out_ref[...] = acc_ref[...].T.astype(BF16)


def project(fields, w):
    variables, rows, columns = fields.shape
    width = w.shape[2]
    return pl.pallas_call(
        project_kernel,
        in_specs=[VMEM_SPEC] * 2,
        out_specs=VMEM_SPEC,
        out_shape=jax.ShapeDtypeStruct((columns, width), BF16),
        scratch_shapes=[pltpu.VMEM((width, columns), F32)],
        compiler_params=params(K3_MIB),
        cost_estimate=pl.CostEstimate(flops=2 * variables * rows * columns * 256,
                                      bytes_accessed=variables * rows * columns * 2, transcendentals=0),
        name="project",
    )(fields, w)


def split3(x):
    high = x.astype(BF16)
    rest = x - high.astype(F32)
    mid = rest.astype(BF16)
    return high, mid, (rest - mid.astype(F32)).astype(BF16)


def inverse_factor_of(width, gram_ref, out_ref, a_ref):
    size = 16
    packed = gram_ref[...]
    a_ref[...] = jnp.zeros_like(a_ref)
    a_ref[:, :128] = packed[:width]
    a_ref[:128, 128:width] = packed[128:width].T
    a_ref[128:, 128:width] = packed[width:, :width - 128]
    a_ref[:, 256:] = jnp.where(
        lax.broadcasted_iota(jnp.int32, (width, 256), 0) == lax.broadcasted_iota(jnp.int32, (width, 256), 1),
        1.0, 0.0)
    row = lax.broadcasted_iota(jnp.int32, (size, 128), 0)
    lane = lax.broadcasted_iota(jnp.int32, (size, 256), 1)
    for start in range(0, width, size):
        panels = [a_ref[start:start + size, tile * 128:(tile + 1) * 128] for tile in range(4)]
        tile, offset = start // 128, start % 128
        cols = [jnp.broadcast_to(panels[tile][:, offset + j:offset + j + 1], (size, 128)) for j in range(size)]
        for j in range(size):
            pivot = jnp.broadcast_to(cols[j][j:j + 1, :], (size, 128))
            inv = lax.rsqrt(pivot)
            inv = inv * (1.5 - 0.5 * pivot * inv * inv)
            low = cols[j] * inv
            for i in range(j + 1, size):
                cols[i] = cols[i] - low * jnp.broadcast_to(low[i:i + 1, :], (size, 128))
            below = jnp.where(row > j, low, 0.0)
            for p in range(4):
                lead = jnp.broadcast_to(panels[p][j:j + 1, :], (size, 128)) * inv
                panels[p] = jnp.where(row == j, lead, panels[p] - below * lead)
        out_ref[start:start + size, :] = jnp.concatenate([panels[2], panels[3]], axis=1)[:, :width]
        if start + size < width:
            whole = jnp.concatenate(panels, axis=1)
            left = jnp.where(lane >= start + size, whole[:, :256], 0.0)
            lh, lm, ll = split3(left)
            rh, rm, rl = split3(whole)
            lhs = jnp.concatenate([lh, lh, lm, lm, lh, ll], axis=0)
            rhs = jnp.concatenate([rh, rm, rh, rm, rl, rh], axis=0)
            update = lax.dot_general(lhs, rhs, (((0,), (0,)), ((), ())), preferred_element_type=F32)
            a_ref[start + size:, :] -= update[start + size:width, :]


def basis_kernel(scale, gram_ref, z_hbm, out_hbm, inv_ref, a_ref, high_ref, low_ref, z_ref, out_ref, z_sem, sems):
    width = z_ref.shape[1]
    blocks = sems.shape[0]
    rows = z_ref.shape[0] // blocks
    z_copy = pltpu.make_async_copy(z_hbm, z_ref, z_sem)
    z_copy.start()
    inverse_factor_of(width, gram_ref, inv_ref, a_ref)
    turned = inv_ref[...].T * scale
    high_ref[...] = turned.astype(BF16)
    low_ref[...] = (turned - high_ref[...].astype(F32)).astype(BF16)
    z_copy.wait()

    def copy_of(i):
        at = pl.ds(pl.multiple_of(i * rows, rows), rows)
        return pltpu.make_async_copy(out_ref.at[at], out_hbm.at[at], sems.at[i])

    def one_block(i, carry):
        at = pl.ds(pl.multiple_of(i * rows, rows), rows)
        z = z_ref[at]
        out_ref[at] = (jnp.dot(z, low_ref[...], preferred_element_type=F32)
                       + jnp.dot(z, high_ref[...], preferred_element_type=F32))
        copy_of(i).start()
        return carry

    lax.fori_loop(0, blocks, one_block, 0)
    for i in range(blocks):
        copy_of(i).wait()


def basis_of(z, gram, scale):
    rows, width = z.shape
    return pl.pallas_call(
        functools.partial(basis_kernel, scale),
        in_specs=[VMEM_SPEC, HBM_SPEC],
        out_specs=[HBM_SPEC, VMEM_SPEC],
        out_shape=[pltpu.HBM((rows, width), F32), jax.ShapeDtypeStruct((width, width), F32)],
        scratch_shapes=[pltpu.VMEM((width, 512), F32), pltpu.VMEM((width, width), BF16),
                        pltpu.VMEM((width, width), BF16), pltpu.VMEM((rows, width), BF16),
                        pltpu.VMEM((rows, width), F32), pltpu.SemaphoreType.DMA,
                        pltpu.SemaphoreType.DMA((K4_BLOCKS,))],
        compiler_params=params(K4_MIB),
        cost_estimate=pl.CostEstimate(flops=1000, bytes_accessed=1000, transcendentals=0),
        name="basis",
    )(gram, in_hbm(z))


def coefficients_kernel(scale, parts_ref, inv_ref, out_ref):
    owned = jnp.sum(parts_ref[...].astype(F32), axis=0)
    out_ref[...] = lax.dot_general(owned, inv_ref[...], (((1,), (1,)), ((), ())),
                                   precision=lax.Precision.HIGHEST, preferred_element_type=F32) * scale


def coefficients_of(parts, inv, scale):
    _, rows, width = parts.shape
    return pl.pallas_call(
        functools.partial(coefficients_kernel, scale),
        in_specs=[pl.BlockSpec(memory_space=pltpu.VMEM)] * 2,
        out_specs=pl.BlockSpec(memory_space=pltpu.VMEM),
        out_shape=jax.ShapeDtypeStruct((rows, width), F32),
        compiler_params=params(32),
        name="coefficients",
    )(parts, inv)


def reduce_all(x, meanwhile):
    passages, layers = lax.axis_size("passage"), lax.axis_size("span")

    def exchange(x, axis, length, moves, meanwhile=None):
        parts = [lax.ppermute(x, axis, [(i, move(i)) for i in range(length)]) for move in moves]
        if meanwhile is not None:
            parts, meanwhile = lax.optimization_barrier((parts, meanwhile))
        for part in parts:
            x = x + part
        return x, meanwhile

    x, _ = exchange(x, "passage", passages, [lambda i: i ^ 1])
    x, meanwhile = exchange(x, "passage", passages, [lambda i, k=k: (i + 2 * k) % passages for k in (1, 3, 2)],
                            meanwhile)
    x, _ = exchange(x, "span", layers, [lambda i, k=k: i // 4 * 4 + (i + k) % 4 for k in (1, 3, 2)])
    x, _ = exchange(x, "span", layers, [lambda i, k=k: (i + 4 * k) % layers for k in (1, 3, 2)])
    return x, meanwhile


def shards(snapshots, sketch, blade_row, row_speed, stencil_reach):
    variables, cells, lines, columns = snapshots.shape
    width = sketch.shape[1]
    passages, layers = lax.axis_size("passage"), lax.axis_size("span")
    row_total = 3 * variables * cells * passages * lines * layers
    fields, y, first_t, last_t, first_r, last_r = fields_and_sketch(
        snapshots.reshape(variables, cells * lines, columns), sketch.T, blade_row, row_speed,
        lines, lines * layers)
    ring_up = [(i, (i + 1) % passages) for i in range(passages)]
    ring_down = [(j, i) for i, j in ring_up]
    line_up = [(i, i + 1) for i in range(layers - 1)]
    line_down = [(j, i) for i, j in line_up]
    before_r = lax.ppermute(last_r, "span", line_up)
    after_r = lax.ppermute(first_r, "span", line_down)
    before_t = lax.ppermute(last_t, "passage", ring_up)
    after_t = lax.ppermute(first_t, "passage", ring_down)
    reach = jnp.broadcast_to(stencil_reach[:, None], (lines, width))
    z, w, gram = stencils(y, before_t, after_t, before_r, after_r, reach, lines)
    projected = project(fields, w)
    gram, projected = reduce_all(gram, projected)
    owned = columns // (passages * layers)
    parts = lax.all_to_all(projected.reshape(passages * layers, owned, width), ("passage", "span"), 0, 0, tiled=True)
    basis, inv = basis_of(z.reshape(-1, width), gram, math.sqrt(row_total))
    coefficients = coefficients_of(parts, inv, 1.0 / math.sqrt(row_total))
    return basis.reshape(3 * variables, cells, lines, width), coefficients


def solution(mesh):
    return jax.shard_map(
        shards,
        mesh=mesh,
        in_specs=(P(None, "passage", "span", None), P(), P("passage"), P(), P("span")),
        out_specs=(P(None, "passage", "span", None), P(("passage", "span"), None)),
        check_vma=False,
    )
```

```python
import functools
import math

import jax
import jax.numpy as jnp
from jax import lax
from jax.experimental import pallas as pl
from jax.experimental.pallas import tpu as pltpu
from jax.sharding import PartitionSpec as P

F32 = jnp.float32
BF16 = jnp.bfloat16
MIB = 1024 * 1024
K1_MIB = 24
K1_CHUNKS = 8
K4_BLOCKS = 5
K2_MIB = 24
K3_MIB = 24
K4_MIB = 24


def in_hbm(x):
    return pltpu.with_memory_space_constraint(x, pltpu.HBM)


def params(mib, **kw):
    return pltpu.CompilerParams(vmem_limit_bytes=mib * MIB, **kw)


def packed_rows(rows, groups):
    return rows + rows // groups


def pack(dst_ref, v, value, groups):
    rows, width = value.shape
    part = rows // groups
    rest = value[:, 128:]
    tail = [rest[g * part:(g + 1) * part] for g in range(groups)]
    spare = 128 - groups * (width - 128)
    if spare:
        tail.append(jnp.zeros((part, spare), value.dtype))
    dst_ref[v, :rows] = value[:, :128].astype(BF16)
    dst_ref[v, rows:] = jnp.concatenate(tail, axis=1).astype(BF16)


def unpack(dst_ref, src_ref, v, groups):
    rows, width = dst_ref.shape
    part = rows // groups
    extra = width - 128
    dst_ref[:, :128] = src_ref[v, :rows].astype(F32)
    rest = src_ref[v, rows:].astype(F32)
    for g in range(groups):
        dst_ref[g * part:(g + 1) * part, 128:] = rest[:, g * extra:(g + 1) * extra]


T_GROUPS = 6
R_GROUPS = 4
VMEM_SPEC = pl.BlockSpec(memory_space=pltpu.VMEM)
HBM_SPEC = pl.BlockSpec(memory_space=pltpu.HBM)


def fields_kernel(radial_total, lines, blade_hbm, speed_hbm, sketch_hbm, snap_hbm,
                  field_ref, y_ref, first_t_ref, last_t_ref, first_r_ref, last_r_ref,
                  blade_ref, speed_ref, sketch_ref, turned_ref, low_r_ref, high_r_ref, small_sems, sems):
    variables, rows, columns = field_ref.shape
    chunks = sems.shape[0]
    part = rows // chunks
    group = 2 * lines
    cells = part // lines
    spare = rows // lines
    small = [pltpu.make_async_copy(blade_hbm, blade_ref, small_sems.at[0]),
             pltpu.make_async_copy(speed_hbm, speed_ref, small_sems.at[1]),
             pltpu.make_async_copy(sketch_hbm, sketch_ref, small_sems.at[2])]
    for copy in small:
        copy.start()

    def copy_of(c):
        at = pl.ds(pl.multiple_of(c * part, part), part)
        return pltpu.make_async_copy(snap_hbm.at[:, at], field_ref.at[:, at], sems.at[c])

    for c in range(chunks):
        copy_of(c).start()
    row_id = lax.broadcasted_iota(jnp.int32, (group, 128), 0)
    line_id = jnp.where(row_id >= lines, row_id - lines, row_id)
    radial_pos = (lax.axis_index("span") * lines + line_id).astype(F32)
    radius = 0.6 + 0.4 * (radial_pos + 0.5) / radial_total
    for copy in small:
        copy.wait()
    turned_ref[...] = sketch_ref[...].T

    def column_speed(cell):
        label = blade_ref[cell]
        total = jnp.float32(0.0)
        for row in range(speed_ref.shape[0]):
            total = jnp.where(label == row, speed_ref[row], total)
        return total

    def one_chunk(c, carry):
        copy_of(c).wait()
        base = pl.multiple_of(c * part, part)
        def one_pair(pair, carry):
            cell = c * cells + 2 * pair
            speed = jnp.where(row_id < lines, column_speed(cell), column_speed(cell + 1))
            shift = speed * radius
            at = pl.ds(pl.multiple_of(base + pair * group, group), group)
            for tile in range(columns // 128):
                lanes = pl.ds(tile * 128, 128)
                density = field_ref[0, at, lanes].astype(F32)
                axial = field_ref[1, at, lanes].astype(F32)
                swirl = field_ref[2, at, lanes].astype(F32) + shift
                radial = field_ref[3, at, lanes].astype(F32)
                kinetic = axial * axial + swirl * swirl + radial * radial
                press = (field_ref[4, at, lanes].astype(F32)
                         + 0.05 * (1.0 + 0.2 * jnp.tanh(density)) * kinetic)
                field_ref[2, at, lanes] = swirl.astype(BF16)
                field_ref[4, at, lanes] = press.astype(BF16)
            return carry

        lax.fori_loop(0, part // group, one_pair, 0)
        block = pl.ds(base, part)
        y = jnp.dot(field_ref[:, block].reshape(variables * part, columns), turned_ref[...],
                    preferred_element_type=F32)
        for v in range(variables):
            y_ref[v, block] = y[v * part:(v + 1) * part]
            for cell in range(cells):
                for side in range(2):
                    to = pl.ds(side * spare + c * cells + cell, 1)
                    row = v * part + cell * lines + side
                    low_r_ref[v, to] = y[row:row + 1]
                    row = row + lines - 2
                    high_r_ref[v, to] = y[row:row + 1]
        return carry

    lax.fori_loop(0, chunks, one_chunk, 0)
    for v in range(variables):
        pack(first_t_ref, v, y_ref[v, :4 * lines], T_GROUPS)
        pack(last_t_ref, v, y_ref[v, rows - 4 * lines:], T_GROUPS)
        pack(first_r_ref, v, low_r_ref[v], R_GROUPS)
        pack(last_r_ref, v, high_r_ref[v], R_GROUPS)


def fields_and_sketch(snapshots, sketch_t, blade_row, row_speed, lines, radial_total):
    variables, rows, columns = snapshots.shape
    width = sketch_t.shape[0]
    chunks = K1_CHUNKS
    cells = rows // lines
    edge_t = jax.ShapeDtypeStruct((variables, packed_rows(4 * lines, T_GROUPS), 128), BF16)
    edge_r = jax.ShapeDtypeStruct((variables, packed_rows(2 * cells, R_GROUPS), 128), BF16)
    return pl.pallas_call(
        functools.partial(fields_kernel, radial_total, lines),
        in_specs=[HBM_SPEC] * 4,
        out_specs=[VMEM_SPEC] * 6,
        out_shape=[
            jax.ShapeDtypeStruct((variables, rows, columns), BF16),
            jax.ShapeDtypeStruct((variables, rows, width), F32),
            edge_t, edge_t, edge_r, edge_r,
        ],
        scratch_shapes=[
            pltpu.SMEM(blade_row.shape, blade_row.dtype),
            pltpu.SMEM(row_speed.shape, row_speed.dtype),
            pltpu.VMEM(sketch_t.shape, sketch_t.dtype),
            pltpu.VMEM(sketch_t.shape[::-1], sketch_t.dtype),
            pltpu.VMEM((variables, 2 * cells, width), F32),
            pltpu.VMEM((variables, 2 * cells, width), F32),
            pltpu.SemaphoreType.DMA((3,)),
            pltpu.SemaphoreType.DMA((chunks,)),
        ],
        compiler_params=params(K1_MIB),
        name="fields_sketch",
    )(in_hbm(blade_row), in_hbm(row_speed), in_hbm(sketch_t), in_hbm(snapshots))


def rounded(x):
    return x.astype(BF16).astype(F32)


def shift_down(x, end):
    return jnp.where(lax.broadcasted_iota(jnp.int32, x.shape, 0) == 0, end, pltpu.roll(x, 1, 0))


def shift_up(x, end):
    last = x.shape[0] - 1
    return jnp.where(lax.broadcasted_iota(jnp.int32, x.shape, 0) == last, end, pltpu.roll(x, last, 0))


def turn(wide, scale, get, t):
    return scale * jnp.where(wide, get(t + 2) - get(t - 2), get(t + 1) - get(t - 1))


def inner_kernel(lines, reach_ref, y_ref, z_out, z_ref, gram_ref, sems):
    variables, rows, width = y_ref.shape
    cells = rows // lines
    wide = reach_ref[...] == 2
    scale = jnp.where(wide, 0.25, 0.5)
    inner = pl.ds(2 * lines, rows - 4 * lines)

    def copies_of(v):
        return [pltpu.make_async_copy(z_ref.at[0, v], z_out.at[0, v], sems.at[0, v]),
                pltpu.make_async_copy(z_ref.at[1, v, inner], z_out.at[1, v, inner], sems.at[1, v])]

    gram_ref[...] = jnp.zeros_like(gram_ref)

    def one_variable(v, carry):
        def y_at(t):
            return y_ref[v, t * lines:(t + 1) * lines, :]

        for pair in range(cells // 2):
            at = pl.ds(2 * pair * lines, 2 * lines)
            z_ref[0, v, at, :] = y_ref[v, at, :].astype(BF16)
            if 0 < pair < cells // 2 - 1:
                z1 = [turn(wide, scale, y_at, t) for t in (2 * pair, 2 * pair + 1)]
                z_ref[1, v, at, :] = jnp.concatenate(z1, axis=0).astype(BF16)
        for z in (z_ref[0, v], z_ref[1, v, inner]):
            gram_ref[...] += lax.dot_general(z, z, (((0,), (0,)), ((), ())), preferred_element_type=F32)
        for copy in copies_of(v):
            copy.start()
        return carry

    lax.fori_loop(0, variables, one_variable, 0)
    for v in range(variables):
        for copy in copies_of(v):
            copy.wait()


def inner_stencils(y, reach, lines):
    variables, rows, width = y.shape
    return pl.pallas_call(
        functools.partial(inner_kernel, lines),
        in_specs=[VMEM_SPEC] * 2,
        out_specs=[HBM_SPEC, VMEM_SPEC, VMEM_SPEC],
        out_shape=[
            pltpu.HBM((2, variables, rows, width), BF16),
            jax.ShapeDtypeStruct((2, variables, rows, width), BF16),
            jax.ShapeDtypeStruct((width, width), F32),
        ],
        scratch_shapes=[pltpu.SemaphoreType.DMA((2, variables))],
        compiler_params=params(16),
        cost_estimate=pl.CostEstimate(flops=4 * variables * rows * 256 * 256, bytes_accessed=variables * rows * 2048,
                                      transcendentals=0),
        name="inner_stencils",
    )(reach, y)


def outer_kernel(lines, reach_ref, y_ref, before_t_in, after_t_in, before_r_in, after_r_in, inner_gram_ref,
                 rim_out, z_out, z_ref, edge_t_ref, edge_r_ref, gram_ref,
                 acc_ref, before_t_ref, after_t_ref, before_r_ref, after_r_ref, rim_ref, sems):
    variables, rows, width = y_ref.shape
    cells = rows // lines
    wide = reach_ref[...] == 2
    scale = jnp.where(wide, 0.25, 0.5)
    span = lax.axis_index("span")
    has_before = jnp.where(span > 0, 0.5, 0.0).astype(F32)
    has_after = jnp.where(span < lax.axis_size("span") - 1, 0.5, 0.0).astype(F32)

    def copies_of(v):
        return [pltpu.make_async_copy(rim_ref.at[v], rim_out.at[v], sems.at[0, v]),
                pltpu.make_async_copy(z_ref.at[v], z_out.at[v], sems.at[1, v])]

    acc_ref[...] = inner_gram_ref[...]

    def one_variable(v, carry):
        unpack(before_t_ref, before_t_in, v, T_GROUPS)
        unpack(after_t_ref, after_t_in, v, T_GROUPS)
        unpack(before_r_ref, before_r_in, v, R_GROUPS)
        unpack(after_r_ref, after_r_in, v, R_GROUPS)

        def y_at(t):
            if t < 0:
                return before_t_ref[(t + 4) * lines:(t + 5) * lines, :]
            if t >= cells:
                return after_t_ref[(t - cells) * lines:(t - cells + 1) * lines, :]
            return y_ref[v, t * lines:(t + 1) * lines, :]

        rim = [turn(wide, scale, y_at, t) for t in RIM_FIRST + tuple(cells + t for t in RIM_LAST)]
        for k, slab in enumerate(rim):
            edge_t_ref[v, k] = rounded(slab)
        rim_ref[v] = jnp.concatenate(rim[2:6], axis=0).astype(BF16)
        for pair in range(cells // 2):
            kept = []
            for t in (2 * pair, 2 * pair + 1):
                y = y_at(t)
                one, two = slice(t, t + 1), slice(cells + t, cells + t + 1)
                edge_r_ref[v, one, :] = rounded(has_before * (y[0:1] - before_r_ref[one, :]))
                edge_r_ref[v, two, :] = rounded(has_after * (after_r_ref[two, :] - y[lines - 1:lines]))
                kept.append(0.5 * (shift_up(y, after_r_ref[one, :]) - shift_down(y, before_r_ref[two, :])))
            z_ref[v, pl.ds(2 * pair * lines, 2 * lines), :] = jnp.concatenate(kept, axis=0).astype(BF16)
        for z in (rim_ref[v], z_ref[v]):
            acc_ref[...] += lax.dot_general(z, z, (((0,), (0,)), ((), ())), preferred_element_type=F32)
        for copy in copies_of(v):
            copy.start()
        return carry

    lax.fori_loop(0, variables, one_variable, 0)
    gram_ref[:width, :] = acc_ref[:, :128]
    gram_ref[width:, :] = jnp.zeros((gram_ref.shape[0] - width, 128), F32)
    gram_ref[width:, :width - 128] = acc_ref[128:, 128:]
    for v in range(variables):
        for copy in copies_of(v):
            copy.wait()


RIM_FIRST = (-2, -1, 0, 1)
RIM_LAST = (-2, -1, 0, 1)


def outer_stencils(y, before_t, after_t, before_r, after_r, inner_gram, reach, lines):
    variables, rows, width = y.shape
    cells = rows // lines
    return pl.pallas_call(
        functools.partial(outer_kernel, lines),
        in_specs=[VMEM_SPEC] * 7,
        out_specs=[HBM_SPEC] * 2 + [VMEM_SPEC] * 4,
        out_shape=[
            pltpu.HBM((variables, 4 * lines, width), BF16),
            pltpu.HBM((variables, rows, width), BF16),
            jax.ShapeDtypeStruct((variables, rows, width), BF16),
            jax.ShapeDtypeStruct((variables, 8, lines, width), F32),
            jax.ShapeDtypeStruct((variables, 2 * cells, width), F32),
            jax.ShapeDtypeStruct((width + (width - 128), 128), F32),
        ],
        scratch_shapes=[
            pltpu.VMEM((width, width), F32),
            pltpu.VMEM((4 * lines, width), F32),
            pltpu.VMEM((4 * lines, width), F32),
            pltpu.VMEM((2 * cells, width), F32),
            pltpu.VMEM((2 * cells, width), F32),
            pltpu.VMEM((variables, 4 * lines, width), BF16),
            pltpu.SemaphoreType.DMA((2, variables)),
        ],
        compiler_params=params(K2_MIB),
        name="outer_stencils",
    )(reach, y, before_t, after_t, before_r, after_r, inner_gram)


def transposed_kernel(lines, reach_ref, z_ref, z2_ref, edge_t_ref, edge_r_ref, w_ref):
    _, variables, rows, width = z_ref.shape
    cells = rows // lines
    wide = reach_ref[...] == 2
    scale = jnp.where(wide, 0.25, 0.5)

    def one_variable(v, carry):
        slabs = {}

        def z1_at(t):
            if t < 2:
                return edge_t_ref[v, t + 2]
            if t >= cells - 2:
                return edge_t_ref[v, t - cells + 6]
            if t not in slabs:
                first = t - t % 2
                both = z_ref[1, v, first * lines:(first + 2) * lines, :].astype(F32)
                slabs[first], slabs[first + 1] = both[:lines], both[lines:]
            return slabs[t]

        for pair in range(cells // 2):
            at = slice(2 * pair * lines, 2 * (pair + 1) * lines)
            z0 = z_ref[0, v, at, :].astype(F32)
            z2 = z2_ref[v, at, :].astype(F32)
            out = []
            for k in range(2):
                t = 2 * pair + k
                part = slice(k * lines, (k + 1) * lines)
                w2 = (shift_down(z2[part], edge_r_ref[v, t:t + 1, :])
                      - shift_up(z2[part], edge_r_ref[v, cells + t:cells + t + 1, :]))
                out.append(z0[part] - turn(wide, scale, z1_at, t) + 0.5 * w2)
            w_ref[v, at, :] = jnp.concatenate(out, axis=0).astype(BF16)
        return carry

    lax.fori_loop(0, variables, one_variable, 0)


def transposed_stencils(z, z2, edge_t, edge_r, reach, lines):
    _, variables, rows, width = z.shape
    return pl.pallas_call(
        functools.partial(transposed_kernel, lines),
        in_specs=[VMEM_SPEC] * 5,
        out_specs=VMEM_SPEC,
        out_shape=jax.ShapeDtypeStruct((variables, rows, width), BF16),
        compiler_params=params(16),
        name="transposed_stencils",
    )(reach, z, z2, edge_t, edge_r)


def project_kernel(field_ref, w_ref, out_ref, acc_ref):
    for v in range(field_ref.shape[0]):
        part = lax.dot_general(w_ref[v], field_ref[v], (((0,), (0,)), ((), ())), preferred_element_type=F32)
        acc_ref[...] = part if v == 0 else acc_ref[...] + part
    out_ref[...] = acc_ref[...].T.astype(BF16)


def project(fields, w):
    variables, rows, columns = fields.shape
    width = w.shape[2]
    return pl.pallas_call(
        project_kernel,
        in_specs=[VMEM_SPEC] * 2,
        out_specs=VMEM_SPEC,
        out_shape=jax.ShapeDtypeStruct((columns, width), BF16),
        scratch_shapes=[pltpu.VMEM((width, columns), F32)],
        compiler_params=params(K3_MIB),
        cost_estimate=pl.CostEstimate(flops=2 * variables * rows * columns * 256,
                                      bytes_accessed=variables * rows * columns * 2, transcendentals=0),
        name="project",
    )(fields, w)


def split3(x):
    high = x.astype(BF16)
    rest = x - high.astype(F32)
    mid = rest.astype(BF16)
    return high, mid, (rest - mid.astype(F32)).astype(BF16)


def inverse_factor_of(width, gram_ref, out_ref, a_ref):
    size = 16
    packed = gram_ref[...]
    a_ref[...] = jnp.zeros_like(a_ref)
    a_ref[:, :128] = packed[:width]
    a_ref[:128, 128:width] = packed[128:width].T
    a_ref[128:, 128:width] = packed[width:, :width - 128]
    a_ref[:, 256:] = jnp.where(
        lax.broadcasted_iota(jnp.int32, (width, 256), 0) == lax.broadcasted_iota(jnp.int32, (width, 256), 1),
        1.0, 0.0)
    row = lax.broadcasted_iota(jnp.int32, (size, 128), 0)
    lane = lax.broadcasted_iota(jnp.int32, (size, 256), 1)
    for start in range(0, width, size):
        panels = [a_ref[start:start + size, tile * 128:(tile + 1) * 128] for tile in range(4)]
        tile, offset = start // 128, start % 128
        cols = [jnp.broadcast_to(panels[tile][:, offset + j:offset + j + 1], (size, 128)) for j in range(size)]
        for j in range(size):
            pivot = jnp.broadcast_to(cols[j][j:j + 1, :], (size, 128))
            inv = lax.rsqrt(pivot)
            inv = inv * (1.5 - 0.5 * pivot * inv * inv)
            low = cols[j] * inv
            for i in range(j + 1, size):
                cols[i] = cols[i] - low * jnp.broadcast_to(low[i:i + 1, :], (size, 128))
            below = jnp.where(row > j, low, 0.0)
            for p in range(4):
                lead = jnp.broadcast_to(panels[p][j:j + 1, :], (size, 128)) * inv
                panels[p] = jnp.where(row == j, lead, panels[p] - below * lead)
        out_ref[start:start + size, :] = jnp.concatenate([panels[2], panels[3]], axis=1)[:, :width]
        if start + size < width:
            whole = jnp.concatenate(panels, axis=1)
            left = jnp.where(lane >= start + size, whole[:, :256], 0.0)
            lh, lm, ll = split3(left)
            rh, rm, rl = split3(whole)
            lhs = jnp.concatenate([lh, lh, lm, lm, lh, ll], axis=0)
            rhs = jnp.concatenate([rh, rm, rh, rm, rl, rh], axis=0)
            update = lax.dot_general(lhs, rhs, (((0,), (0,)), ((), ())), preferred_element_type=F32)
            a_ref[start + size:, :] -= update[start + size:width, :]


def basis_kernel(scale, gram_ref, inner_hbm, rim_hbm, last_hbm, out_hbm, inv_ref, a_ref, high_ref, low_ref,
                 z_ref, out_ref, z_sems, sems):
    width = z_ref.shape[2]
    blocks = sems.shape[0]
    group = z_ref.shape[0] // blocks
    rows = group * z_ref.shape[1]
    variables, rim = rim_hbm.shape[:2]
    cells = last_hbm.shape[1]
    half = rim // 2
    middle = pl.ds(half, cells - rim)
    second = z_ref.at[pl.ds(variables, variables)]
    pieces = [
        (inner_hbm.at[0], z_ref.at[pl.ds(0, variables)]),
        (inner_hbm.at[1, :, middle], second.at[:, middle]),
        (rim_hbm.at[:, pl.ds(0, half)], second.at[:, pl.ds(0, half)]),
        (rim_hbm.at[:, pl.ds(half, half)], second.at[:, pl.ds(cells - half, half)]),
        (last_hbm, z_ref.at[pl.ds(2 * variables, variables)]),
    ]
    z_copies = [pltpu.make_async_copy(source, target, z_sems.at[k]) for k, (source, target) in enumerate(pieces)]
    for copy in z_copies:
        copy.start()
    inverse_factor_of(width, gram_ref, inv_ref, a_ref)
    turned = inv_ref[...].T * scale
    high_ref[...] = turned.astype(BF16)
    low_ref[...] = (turned - high_ref[...].astype(F32)).astype(BF16)
    for copy in z_copies:
        copy.wait()

    def copy_of(i):
        at = pl.ds(pl.multiple_of(i * rows, rows), rows)
        return pltpu.make_async_copy(out_ref.at[at], out_hbm.at[at], sems.at[i])

    def one_block(i, carry):
        at = pl.ds(pl.multiple_of(i * rows, rows), rows)
        z = z_ref[pl.ds(i * group, group)].reshape(rows, width)
        out_ref[at] = (jnp.dot(z, low_ref[...], preferred_element_type=F32)
                       + jnp.dot(z, high_ref[...], preferred_element_type=F32))
        copy_of(i).start()
        return carry

    lax.fori_loop(0, blocks, one_block, 0)
    for i in range(blocks):
        copy_of(i).wait()


def basis_of(inner, rim, last, gram, scale):
    variables, cells, width = last.shape
    rows = 3 * variables * cells
    return pl.pallas_call(
        functools.partial(basis_kernel, scale),
        in_specs=[VMEM_SPEC] + [HBM_SPEC] * 3,
        out_specs=[HBM_SPEC, VMEM_SPEC],
        out_shape=[pltpu.HBM((rows, width), F32), jax.ShapeDtypeStruct((width, width), F32)],
        scratch_shapes=[pltpu.VMEM((width, 512), F32), pltpu.VMEM((width, width), BF16),
                        pltpu.VMEM((width, width), BF16), pltpu.VMEM((3 * variables, cells, width), BF16),
                        pltpu.VMEM((rows, width), F32), pltpu.SemaphoreType.DMA((5,)),
                        pltpu.SemaphoreType.DMA((K4_BLOCKS,))],
        compiler_params=params(K4_MIB),
        cost_estimate=pl.CostEstimate(flops=1000, bytes_accessed=1000, transcendentals=0),
        name="basis",
    )(gram, in_hbm(inner), in_hbm(rim), in_hbm(last))


def coefficients_kernel(scale, parts_ref, inv_ref, out_ref):
    owned = jnp.sum(parts_ref[...].astype(F32), axis=0)
    out_ref[...] = lax.dot_general(owned, inv_ref[...], (((1,), (1,)), ((), ())),
                                   precision=lax.Precision.HIGHEST, preferred_element_type=F32) * scale


def coefficients_of(parts, inv, scale):
    _, rows, width = parts.shape
    return pl.pallas_call(
        functools.partial(coefficients_kernel, scale),
        in_specs=[pl.BlockSpec(memory_space=pltpu.VMEM)] * 2,
        out_specs=pl.BlockSpec(memory_space=pltpu.VMEM),
        out_shape=jax.ShapeDtypeStruct((rows, width), F32),
        compiler_params=params(32),
        name="coefficients",
    )(parts, inv)


def reduce_all(x, start, finish):
    passages, layers = lax.axis_size("passage"), lax.axis_size("span")

    def exchange(x, axis, length, moves, meanwhile=None):
        parts = [lax.ppermute(x, axis, [(i, move(i)) for i in range(length)]) for move in moves]
        if meanwhile is not None:
            parts, meanwhile = lax.optimization_barrier((parts, meanwhile))
        for part in parts:
            x = x + part
        return x, meanwhile

    w = start()
    x, w = exchange(x, "passage", passages, [lambda i, k=k: (i + 2 * k) % passages for k in (1, 3, 2)], w)
    projected = finish(w)
    x, projected = exchange(x, "span", layers, [lambda i, k=k: i // 4 * 4 + (i + k) % 4 for k in (1, 3, 2)],
                            projected)
    x, _ = exchange(x, "span", layers, [lambda i, k=k: (i + 4 * k) % layers for k in (1, 3, 2)])
    x, _ = exchange(x, "passage", passages, [lambda i: i ^ 1])
    return x, projected


def shards(snapshots, sketch, blade_row, row_speed, stencil_reach):
    variables, cells, lines, columns = snapshots.shape
    width = sketch.shape[1]
    passages, layers = lax.axis_size("passage"), lax.axis_size("span")
    row_total = 3 * variables * cells * passages * lines * layers
    fields, y, first_t, last_t, first_r, last_r = fields_and_sketch(
        snapshots.reshape(variables, cells * lines, columns), sketch.T, blade_row, row_speed,
        lines, lines * layers)
    ring_up = [(i, (i + 1) % passages) for i in range(passages)]
    ring_down = [(j, i) for i, j in ring_up]
    line_up = [(i, i + 1) for i in range(layers - 1)]
    line_down = [(j, i) for i, j in line_up]
    before_r = lax.ppermute(last_r, "span", line_up)
    after_r = lax.ppermute(first_r, "span", line_down)
    before_t = lax.ppermute(last_t, "passage", ring_up)
    after_t = lax.ppermute(first_t, "passage", ring_down)
    reach = jnp.broadcast_to(stencil_reach[:, None], (lines, width))
    inner, held, inner_gram = inner_stencils(y, reach, lines)
    halos, inner_gram = lax.optimization_barrier(((before_t, after_t, before_r, after_r), inner_gram))
    rim, last, z2, edge_t, edge_r, gram = outer_stencils(y, *halos, inner_gram, reach, lines)
    gram, projected = reduce_all(
        gram, lambda: transposed_stencils(held, z2, edge_t, edge_r, reach, lines), lambda w: project(fields, w))
    owned = columns // (passages * layers)
    parts = lax.all_to_all(projected.reshape(passages * layers, owned, width), ("passage", "span"), 0, 0, tiled=True)
    basis, inv = basis_of(inner, rim, last, gram, math.sqrt(row_total))
    coefficients = coefficients_of(parts, inv, 1.0 / math.sqrt(row_total))
    return basis.reshape(3 * variables, cells, lines, width), coefficients


def solution(mesh):
    return jax.shard_map(
        shards,
        mesh=mesh,
        in_specs=(P(None, "passage", "span", None), P(), P("passage"), P(), P("span")),
        out_specs=(P(None, "passage", "span", None), P(("passage", "span"), None)),
        check_vma=False,
    )
```

```python
import functools
import math

import jax
import jax.numpy as jnp
from jax import lax
from jax.experimental import pallas as pl
from jax.experimental.pallas import tpu as pltpu
from jax.sharding import PartitionSpec as P

F32 = jnp.float32
BF16 = jnp.bfloat16
MIB = 1024 * 1024
K1_MIB = 24
K1_CHUNKS = 4
K4_BLOCKS = 5
K2_MIB = 24
K3_MIB = 24
K4_MIB = 24


def in_hbm(x):
    return pltpu.with_memory_space_constraint(x, pltpu.HBM)


def params(mib, **kw):
    return pltpu.CompilerParams(vmem_limit_bytes=mib * MIB, **kw)


def packed_rows(rows, groups):
    return rows + rows // groups


def pack(dst_ref, v, value, groups):
    rows, width = value.shape
    part = rows // groups
    rest = value[:, 128:]
    tail = [rest[g * part:(g + 1) * part] for g in range(groups)]
    spare = 128 - groups * (width - 128)
    if spare:
        tail.append(jnp.zeros((part, spare), value.dtype))
    dst_ref[v, :rows] = value[:, :128].astype(BF16)
    dst_ref[v, rows:] = jnp.concatenate(tail, axis=1).astype(BF16)


def unpack(dst_ref, src_ref, v, groups):
    rows, width = dst_ref.shape
    part = rows // groups
    extra = width - 128
    dst_ref[:, :128] = src_ref[v, :rows].astype(F32)
    rest = src_ref[v, rows:].astype(F32)
    for g in range(groups):
        dst_ref[g * part:(g + 1) * part, 128:] = rest[:, g * extra:(g + 1) * extra]


T_GROUPS = 6
R_GROUPS = 4
VMEM_SPEC = pl.BlockSpec(memory_space=pltpu.VMEM)
HBM_SPEC = pl.BlockSpec(memory_space=pltpu.HBM)


def fields_kernel(radial_total, lines, blade_hbm, speed_hbm, sketch_hbm, snap_hbm,
                  field_ref, y_ref, first_t_ref, last_t_ref, first_r_ref, last_r_ref,
                  blade_ref, speed_ref, sketch_ref, turned_ref, low_r_ref, high_r_ref, small_sems, sems):
    variables, rows, columns = field_ref.shape
    chunks = sems.shape[0]
    part = rows // chunks
    group = 2 * lines
    cells = part // lines
    spare = rows // lines
    small = [pltpu.make_async_copy(blade_hbm, blade_ref, small_sems.at[0]),
             pltpu.make_async_copy(speed_hbm, speed_ref, small_sems.at[1]),
             pltpu.make_async_copy(sketch_hbm, sketch_ref, small_sems.at[2])]
    for copy in small:
        copy.start()

    def copy_of(c):
        at = pl.ds(pl.multiple_of(c * part, part), part)
        return pltpu.make_async_copy(snap_hbm.at[:, at], field_ref.at[:, at], sems.at[c])

    for c in range(chunks):
        copy_of(c).start()
    row_id = lax.broadcasted_iota(jnp.int32, (group, 128), 0)
    line_id = jnp.where(row_id >= lines, row_id - lines, row_id)
    radial_pos = (lax.axis_index("span") * lines + line_id).astype(F32)
    radius = 0.6 + 0.4 * (radial_pos + 0.5) / radial_total
    for copy in small:
        copy.wait()
    turned_ref[...] = sketch_ref[...].T

    def column_speed(cell):
        label = blade_ref[cell]
        total = jnp.float32(0.0)
        for row in range(speed_ref.shape[0]):
            total = jnp.where(label == row, speed_ref[row], total)
        return total

    def one_chunk(c, carry):
        copy_of(c).wait()
        base = pl.multiple_of(c * part, part)
        def one_pair(pair, carry):
            cell = c * cells + 2 * pair
            speed = jnp.where(row_id < lines, column_speed(cell), column_speed(cell + 1))
            shift = speed * radius
            at = pl.ds(pl.multiple_of(base + pair * group, group), group)
            for tile in range(columns // 128):
                lanes = pl.ds(tile * 128, 128)
                density = field_ref[0, at, lanes].astype(F32)
                axial = field_ref[1, at, lanes].astype(F32)
                swirl = field_ref[2, at, lanes].astype(F32) + shift
                radial = field_ref[3, at, lanes].astype(F32)
                kinetic = axial * axial + swirl * swirl + radial * radial
                press = (field_ref[4, at, lanes].astype(F32)
                         + 0.05 * (1.0 + 0.2 * jnp.tanh(density)) * kinetic)
                field_ref[2, at, lanes] = swirl.astype(BF16)
                field_ref[4, at, lanes] = press.astype(BF16)
            return carry

        lax.fori_loop(0, part // group, one_pair, 0)
        block = pl.ds(base, part)
        y = jnp.dot(field_ref[:, block].reshape(variables * part, columns), turned_ref[...],
                    preferred_element_type=F32)
        for v in range(variables):
            y_ref[v, block] = y[v * part:(v + 1) * part]
            for cell in range(cells):
                for side in range(2):
                    to = pl.ds(side * spare + c * cells + cell, 1)
                    row = v * part + cell * lines + side
                    low_r_ref[v, to] = y[row:row + 1]
                    row = row + lines - 2
                    high_r_ref[v, to] = y[row:row + 1]
        return carry

    lax.fori_loop(0, chunks, one_chunk, 0)
    for v in range(variables):
        pack(first_t_ref, v, y_ref[v, :4 * lines], T_GROUPS)
        pack(last_t_ref, v, y_ref[v, rows - 4 * lines:], T_GROUPS)
        pack(first_r_ref, v, low_r_ref[v], R_GROUPS)
        pack(last_r_ref, v, high_r_ref[v], R_GROUPS)


def fields_and_sketch(snapshots, sketch_t, blade_row, row_speed, lines, radial_total):
    variables, rows, columns = snapshots.shape
    width = sketch_t.shape[0]
    chunks = K1_CHUNKS
    cells = rows // lines
    edge_t = jax.ShapeDtypeStruct((variables, packed_rows(4 * lines, T_GROUPS), 128), BF16)
    edge_r = jax.ShapeDtypeStruct((variables, packed_rows(2 * cells, R_GROUPS), 128), BF16)
    return pl.pallas_call(
        functools.partial(fields_kernel, radial_total, lines),
        in_specs=[HBM_SPEC] * 4,
        out_specs=[VMEM_SPEC] * 6,
        out_shape=[
            jax.ShapeDtypeStruct((variables, rows, columns), BF16),
            jax.ShapeDtypeStruct((variables, rows, width), F32),
            edge_t, edge_t, edge_r, edge_r,
        ],
        scratch_shapes=[
            pltpu.SMEM(blade_row.shape, blade_row.dtype),
            pltpu.SMEM(row_speed.shape, row_speed.dtype),
            pltpu.VMEM(sketch_t.shape, sketch_t.dtype),
            pltpu.VMEM(sketch_t.shape[::-1], sketch_t.dtype),
            pltpu.VMEM((variables, 2 * cells, width), F32),
            pltpu.VMEM((variables, 2 * cells, width), F32),
            pltpu.SemaphoreType.DMA((3,)),
            pltpu.SemaphoreType.DMA((chunks,)),
        ],
        compiler_params=params(K1_MIB),
        name="fields_sketch",
    )(in_hbm(blade_row), in_hbm(row_speed), in_hbm(sketch_t), in_hbm(snapshots))


def rounded(x):
    return x.astype(BF16).astype(F32)


def shift_down(x, end):
    return jnp.where(lax.broadcasted_iota(jnp.int32, x.shape, 0) == 0, end, pltpu.roll(x, 1, 0))


def shift_up(x, end):
    last = x.shape[0] - 1
    return jnp.where(lax.broadcasted_iota(jnp.int32, x.shape, 0) == last, end, pltpu.roll(x, last, 0))


def turn(wide, scale, get, t):
    return scale * jnp.where(wide, get(t + 2) - get(t - 2), get(t + 1) - get(t - 1))


def inner_kernel(lines, reach_ref, y_ref, z_out, z_ref, gram_ref, sems):
    variables, rows, width = y_ref.shape
    cells = rows // lines
    wide = reach_ref[...] == 2
    scale = jnp.where(wide, 0.25, 0.5)
    inner = pl.ds(2 * lines, rows - 4 * lines)

    def copies_of(v):
        return [pltpu.make_async_copy(z_ref.at[0, v], z_out.at[0, v], sems.at[0, v]),
                pltpu.make_async_copy(z_ref.at[1, v, inner], z_out.at[1, v, inner], sems.at[1, v])]

    gram_ref[...] = jnp.zeros_like(gram_ref)

    def one_variable(v, carry):
        def y_at(t):
            return y_ref[v, t * lines:(t + 1) * lines, :]

        for pair in range(cells // 2):
            at = pl.ds(2 * pair * lines, 2 * lines)
            z_ref[0, v, at, :] = y_ref[v, at, :].astype(BF16)
            if 0 < pair < cells // 2 - 1:
                z1 = [turn(wide, scale, y_at, t) for t in (2 * pair, 2 * pair + 1)]
                z_ref[1, v, at, :] = jnp.concatenate(z1, axis=0).astype(BF16)
        for z in (z_ref[0, v], z_ref[1, v, inner]):
            gram_ref[...] += lax.dot_general(z, z, (((0,), (0,)), ((), ())), preferred_element_type=F32)
        for copy in copies_of(v):
            copy.start()
        return carry

    lax.fori_loop(0, variables, one_variable, 0)
    for v in range(variables):
        for copy in copies_of(v):
            copy.wait()


def inner_stencils(y, reach, lines):
    variables, rows, width = y.shape
    return pl.pallas_call(
        functools.partial(inner_kernel, lines),
        in_specs=[VMEM_SPEC] * 2,
        out_specs=[HBM_SPEC, VMEM_SPEC, VMEM_SPEC],
        out_shape=[
            pltpu.HBM((2, variables, rows, width), BF16),
            jax.ShapeDtypeStruct((2, variables, rows, width), BF16),
            jax.ShapeDtypeStruct((width, width), F32),
        ],
        scratch_shapes=[pltpu.SemaphoreType.DMA((2, variables))],
        compiler_params=params(16),
        cost_estimate=pl.CostEstimate(flops=4 * variables * rows * 256 * 256, bytes_accessed=variables * rows * 2048,
                                      transcendentals=0),
        name="inner_stencils",
    )(reach, y)


def outer_kernel(lines, reach_ref, y_ref, before_t_in, after_t_in, before_r_in, after_r_in, inner_gram_ref,
                 rim_out, z_out, z_ref, edge_t_ref, edge_r_ref, gram_ref,
                 acc_ref, before_t_ref, after_t_ref, before_r_ref, after_r_ref, rim_ref, sems):
    variables, rows, width = y_ref.shape
    cells = rows // lines
    wide = reach_ref[...] == 2
    scale = jnp.where(wide, 0.25, 0.5)
    span = lax.axis_index("span")
    has_before = jnp.where(span > 0, 0.5, 0.0).astype(F32)
    has_after = jnp.where(span < lax.axis_size("span") - 1, 0.5, 0.0).astype(F32)

    def copies_of(v):
        return [pltpu.make_async_copy(rim_ref.at[v], rim_out.at[v], sems.at[0, v]),
                pltpu.make_async_copy(z_ref.at[v], z_out.at[v], sems.at[1, v])]

    acc_ref[...] = inner_gram_ref[...]

    def one_variable(v, carry):
        unpack(before_t_ref, before_t_in, v, T_GROUPS)
        unpack(after_t_ref, after_t_in, v, T_GROUPS)
        unpack(before_r_ref, before_r_in, v, R_GROUPS)
        unpack(after_r_ref, after_r_in, v, R_GROUPS)

        def y_at(t):
            if t < 0:
                return before_t_ref[(t + 4) * lines:(t + 5) * lines, :]
            if t >= cells:
                return after_t_ref[(t - cells) * lines:(t - cells + 1) * lines, :]
            return y_ref[v, t * lines:(t + 1) * lines, :]

        rim = [turn(wide, scale, y_at, t) for t in RIM_FIRST + tuple(cells + t for t in RIM_LAST)]
        for k, slab in enumerate(rim):
            edge_t_ref[v, k] = rounded(slab)
        rim_ref[v] = jnp.concatenate(rim[2:6], axis=0).astype(BF16)
        for pair in range(cells // 2):
            kept = []
            for t in (2 * pair, 2 * pair + 1):
                y = y_at(t)
                one, two = slice(t, t + 1), slice(cells + t, cells + t + 1)
                edge_r_ref[v, one, :] = rounded(has_before * (y[0:1] - before_r_ref[one, :]))
                edge_r_ref[v, two, :] = rounded(has_after * (after_r_ref[two, :] - y[lines - 1:lines]))
                kept.append(0.5 * (shift_up(y, after_r_ref[one, :]) - shift_down(y, before_r_ref[two, :])))
            z_ref[v, pl.ds(2 * pair * lines, 2 * lines), :] = jnp.concatenate(kept, axis=0).astype(BF16)
        for z in (rim_ref[v], z_ref[v]):
            acc_ref[...] += lax.dot_general(z, z, (((0,), (0,)), ((), ())), preferred_element_type=F32)
        for copy in copies_of(v):
            copy.start()
        return carry

    lax.fori_loop(0, variables, one_variable, 0)
    gram_ref[:width, :] = acc_ref[:, :128]
    gram_ref[width:, :] = jnp.zeros((gram_ref.shape[0] - width, 128), F32)
    gram_ref[width:, :width - 128] = acc_ref[128:, 128:]
    for v in range(variables):
        for copy in copies_of(v):
            copy.wait()


RIM_FIRST = (-2, -1, 0, 1)
RIM_LAST = (-2, -1, 0, 1)


def outer_stencils(y, before_t, after_t, before_r, after_r, inner_gram, reach, lines):
    variables, rows, width = y.shape
    cells = rows // lines
    return pl.pallas_call(
        functools.partial(outer_kernel, lines),
        in_specs=[VMEM_SPEC] * 7,
        out_specs=[HBM_SPEC] * 2 + [VMEM_SPEC] * 4,
        out_shape=[
            pltpu.HBM((variables, 4 * lines, width), BF16),
            pltpu.HBM((variables, rows, width), BF16),
            jax.ShapeDtypeStruct((variables, rows, width), BF16),
            jax.ShapeDtypeStruct((variables, 8, lines, width), F32),
            jax.ShapeDtypeStruct((variables, 2 * cells, width), F32),
            jax.ShapeDtypeStruct((width + (width - 128), 128), F32),
        ],
        scratch_shapes=[
            pltpu.VMEM((width, width), F32),
            pltpu.VMEM((4 * lines, width), F32),
            pltpu.VMEM((4 * lines, width), F32),
            pltpu.VMEM((2 * cells, width), F32),
            pltpu.VMEM((2 * cells, width), F32),
            pltpu.VMEM((variables, 4 * lines, width), BF16),
            pltpu.SemaphoreType.DMA((2, variables)),
        ],
        compiler_params=params(K2_MIB),
        name="outer_stencils",
    )(reach, y, before_t, after_t, before_r, after_r, inner_gram)


def transposed_kernel(lines, reach_ref, z_ref, z2_ref, edge_t_ref, edge_r_ref, w_ref):
    _, variables, rows, width = z_ref.shape
    cells = rows // lines
    wide = reach_ref[...] == 2
    scale = jnp.where(wide, 0.25, 0.5)

    def one_variable(v, carry):
        slabs = {}

        def z1_at(t):
            if t < 2:
                return edge_t_ref[v, t + 2]
            if t >= cells - 2:
                return edge_t_ref[v, t - cells + 6]
            if t not in slabs:
                first = t - t % 2
                both = z_ref[1, v, first * lines:(first + 2) * lines, :].astype(F32)
                slabs[first], slabs[first + 1] = both[:lines], both[lines:]
            return slabs[t]

        for pair in range(cells // 2):
            at = slice(2 * pair * lines, 2 * (pair + 1) * lines)
            z0 = z_ref[0, v, at, :].astype(F32)
            z2 = z2_ref[v, at, :].astype(F32)
            out = []
            for k in range(2):
                t = 2 * pair + k
                part = slice(k * lines, (k + 1) * lines)
                w2 = (shift_down(z2[part], edge_r_ref[v, t:t + 1, :])
                      - shift_up(z2[part], edge_r_ref[v, cells + t:cells + t + 1, :]))
                out.append(z0[part] - turn(wide, scale, z1_at, t) + 0.5 * w2)
            w_ref[v, at, :] = jnp.concatenate(out, axis=0).astype(BF16)
        return carry

    lax.fori_loop(0, variables, one_variable, 0)


def transposed_stencils(z, z2, edge_t, edge_r, reach, lines):
    _, variables, rows, width = z.shape
    return pl.pallas_call(
        functools.partial(transposed_kernel, lines),
        in_specs=[VMEM_SPEC] * 5,
        out_specs=VMEM_SPEC,
        out_shape=jax.ShapeDtypeStruct((variables, rows, width), BF16),
        compiler_params=params(16),
        name="transposed_stencils",
    )(reach, z, z2, edge_t, edge_r)


def project_kernel(field_ref, w_ref, out_ref, acc_ref):
    for v in range(field_ref.shape[0]):
        part = lax.dot_general(w_ref[v], field_ref[v], (((0,), (0,)), ((), ())), preferred_element_type=F32)
        acc_ref[...] = part if v == 0 else acc_ref[...] + part
    out_ref[...] = acc_ref[...].T.astype(BF16)


def project(fields, w):
    variables, rows, columns = fields.shape
    width = w.shape[2]
    return pl.pallas_call(
        project_kernel,
        in_specs=[VMEM_SPEC] * 2,
        out_specs=VMEM_SPEC,
        out_shape=jax.ShapeDtypeStruct((columns, width), BF16),
        scratch_shapes=[pltpu.VMEM((width, columns), F32)],
        compiler_params=params(K3_MIB),
        cost_estimate=pl.CostEstimate(flops=2 * variables * rows * columns * 256,
                                      bytes_accessed=variables * rows * columns * 2, transcendentals=0),
        name="project",
    )(fields, w)


def split3(x):
    high = x.astype(BF16)
    rest = x - high.astype(F32)
    mid = rest.astype(BF16)
    return high, mid, (rest - mid.astype(F32)).astype(BF16)


def inverse_factor_of(width, gram_ref, out_ref, a_ref):
    size = 16
    packed = gram_ref[...]
    a_ref[...] = jnp.zeros_like(a_ref)
    a_ref[:, :128] = packed[:width]
    a_ref[:128, 128:width] = packed[128:width].T
    a_ref[128:, 128:width] = packed[width:, :width - 128]
    a_ref[:, 256:] = jnp.where(
        lax.broadcasted_iota(jnp.int32, (width, 256), 0) == lax.broadcasted_iota(jnp.int32, (width, 256), 1),
        1.0, 0.0)
    row = lax.broadcasted_iota(jnp.int32, (size, 128), 0)
    lane = lax.broadcasted_iota(jnp.int32, (size, 256), 1)
    for start in range(0, width, size):
        panels = [a_ref[start:start + size, tile * 128:(tile + 1) * 128] for tile in range(4)]
        tile, offset = start // 128, start % 128
        cols = [jnp.broadcast_to(panels[tile][:, offset + j:offset + j + 1], (size, 128)) for j in range(size)]
        for j in range(size):
            pivot = jnp.broadcast_to(cols[j][j:j + 1, :], (size, 128))
            inv = lax.rsqrt(pivot)
            inv = inv * (1.5 - 0.5 * pivot * inv * inv)
            low = cols[j] * inv
            for i in range(j + 1, size):
                cols[i] = cols[i] - low * jnp.broadcast_to(low[i:i + 1, :], (size, 128))
            below = jnp.where(row > j, low, 0.0)
            for p in range(4):
                lead = jnp.broadcast_to(panels[p][j:j + 1, :], (size, 128)) * inv
                panels[p] = jnp.where(row == j, lead, panels[p] - below * lead)
        out_ref[start:start + size, :] = jnp.concatenate([panels[2], panels[3]], axis=1)[:, :width]
        if start + size < width:
            whole = jnp.concatenate(panels, axis=1)
            left = jnp.where(lane >= start + size, whole[:, :256], 0.0)
            lh, lm, ll = split3(left)
            rh, rm, rl = split3(whole)
            lhs = jnp.concatenate([lh, lh, lm, lm, lh, ll], axis=0)
            rhs = jnp.concatenate([rh, rm, rh, rm, rl, rh], axis=0)
            update = lax.dot_general(lhs, rhs, (((0,), (0,)), ((), ())), preferred_element_type=F32)
            a_ref[start + size:, :] -= update[start + size:width, :]


def basis_kernel(scale, gram_ref, inner_hbm, rim_hbm, last_hbm, out_hbm, inv_ref, a_ref, high_ref, low_ref,
                 z_ref, out_ref, z_sems, sems):
    width = z_ref.shape[2]
    blocks = sems.shape[0]
    group = z_ref.shape[0] // blocks
    rows = group * z_ref.shape[1]
    variables, rim = rim_hbm.shape[:2]
    cells = last_hbm.shape[1]
    half = rim // 2
    middle = pl.ds(half, cells - rim)
    second = z_ref.at[pl.ds(variables, variables)]
    pieces = [
        (inner_hbm.at[0], z_ref.at[pl.ds(0, variables)]),
        (inner_hbm.at[1, :, middle], second.at[:, middle]),
        (rim_hbm.at[:, pl.ds(0, half)], second.at[:, pl.ds(0, half)]),
        (rim_hbm.at[:, pl.ds(half, half)], second.at[:, pl.ds(cells - half, half)]),
        (last_hbm, z_ref.at[pl.ds(2 * variables, variables)]),
    ]
    z_copies = [pltpu.make_async_copy(source, target, z_sems.at[k]) for k, (source, target) in enumerate(pieces)]
    for copy in z_copies:
        copy.start()
    inverse_factor_of(width, gram_ref, inv_ref, a_ref)
    turned = inv_ref[...].T * scale
    high_ref[...] = turned.astype(BF16)
    low_ref[...] = (turned - high_ref[...].astype(F32)).astype(BF16)
    for copy in z_copies:
        copy.wait()

    def copy_of(i):
        at = pl.ds(pl.multiple_of(i * rows, rows), rows)
        return pltpu.make_async_copy(out_ref.at[at], out_hbm.at[at], sems.at[i])

    def one_block(i, carry):
        at = pl.ds(pl.multiple_of(i * rows, rows), rows)
        z = z_ref[pl.ds(i * group, group)].reshape(rows, width)
        out_ref[at] = (jnp.dot(z, low_ref[...], preferred_element_type=F32)
                       + jnp.dot(z, high_ref[...], preferred_element_type=F32))
        copy_of(i).start()
        return carry

    lax.fori_loop(0, blocks, one_block, 0)
    for i in range(blocks):
        copy_of(i).wait()


def basis_of(inner, rim, last, gram, scale):
    variables, cells, width = last.shape
    rows = 3 * variables * cells
    return pl.pallas_call(
        functools.partial(basis_kernel, scale),
        in_specs=[VMEM_SPEC] + [HBM_SPEC] * 3,
        out_specs=[HBM_SPEC, VMEM_SPEC],
        out_shape=[pltpu.HBM((rows, width), F32), jax.ShapeDtypeStruct((width, width), F32)],
        scratch_shapes=[pltpu.VMEM((width, 512), F32), pltpu.VMEM((width, width), BF16),
                        pltpu.VMEM((width, width), BF16), pltpu.VMEM((3 * variables, cells, width), BF16),
                        pltpu.VMEM((rows, width), F32), pltpu.SemaphoreType.DMA((5,)),
                        pltpu.SemaphoreType.DMA((K4_BLOCKS,))],
        compiler_params=params(K4_MIB),
        cost_estimate=pl.CostEstimate(flops=1000, bytes_accessed=1000, transcendentals=0),
        name="basis",
    )(gram, in_hbm(inner), in_hbm(rim), in_hbm(last))


def coefficients_kernel(scale, parts_ref, inv_ref, out_ref):
    owned = jnp.sum(parts_ref[...].astype(F32), axis=0)
    out_ref[...] = lax.dot_general(owned, inv_ref[...], (((1,), (1,)), ((), ())),
                                   precision=lax.Precision.HIGHEST, preferred_element_type=F32) * scale


def coefficients_of(parts, inv, scale):
    _, rows, width = parts.shape
    return pl.pallas_call(
        functools.partial(coefficients_kernel, scale),
        in_specs=[pl.BlockSpec(memory_space=pltpu.VMEM)] * 2,
        out_specs=pl.BlockSpec(memory_space=pltpu.VMEM),
        out_shape=jax.ShapeDtypeStruct((rows, width), F32),
        compiler_params=params(32),
        name="coefficients",
    )(parts, inv)


def reduce_all(x, start, finish):
    passages, layers = lax.axis_size("passage"), lax.axis_size("span")

    def exchange(x, axis, length, moves, meanwhile=None):
        parts = [lax.ppermute(x, axis, [(i, move(i)) for i in range(length)]) for move in moves]
        if meanwhile is not None:
            parts, meanwhile = lax.optimization_barrier((parts, meanwhile))
        for part in parts:
            x = x + part
        return x, meanwhile

    w = start()
    x, w = exchange(x, "passage", passages, [lambda i, k=k: (i + 2 * k) % passages for k in (1, 3, 2)], w)
    projected = finish(w)
    x, projected = exchange(x, "span", layers, [lambda i, k=k: i // 4 * 4 + (i + k) % 4 for k in (1, 3, 2)],
                            projected)
    x, _ = exchange(x, "span", layers, [lambda i, k=k: (i + 4 * k) % layers for k in (1, 3, 2)])
    x, _ = exchange(x, "passage", passages, [lambda i: i ^ 1])
    return x, projected


def shards(snapshots, sketch, blade_row, row_speed, stencil_reach):
    variables, cells, lines, columns = snapshots.shape
    width = sketch.shape[1]
    passages, layers = lax.axis_size("passage"), lax.axis_size("span")
    row_total = 3 * variables * cells * passages * lines * layers
    fields, y, first_t, last_t, first_r, last_r = fields_and_sketch(
        snapshots.reshape(variables, cells * lines, columns), sketch.T, blade_row, row_speed,
        lines, lines * layers)
    ring_up = [(i, (i + 1) % passages) for i in range(passages)]
    ring_down = [(j, i) for i, j in ring_up]
    line_up = [(i, i + 1) for i in range(layers - 1)]
    line_down = [(j, i) for i, j in line_up]
    before_r = lax.ppermute(last_r, "span", line_up)
    after_r = lax.ppermute(first_r, "span", line_down)
    before_t = lax.ppermute(last_t, "passage", ring_up)
    after_t = lax.ppermute(first_t, "passage", ring_down)
    reach = jnp.broadcast_to(stencil_reach[:, None], (lines, width))
    inner, held, inner_gram = inner_stencils(y, reach, lines)
    halos, inner_gram = lax.optimization_barrier(((before_t, after_t, before_r, after_r), inner_gram))
    rim, last, z2, edge_t, edge_r, gram = outer_stencils(y, *halos, inner_gram, reach, lines)
    gram, projected = reduce_all(
        gram, lambda: transposed_stencils(held, z2, edge_t, edge_r, reach, lines), lambda w: project(fields, w))
    owned = columns // (passages * layers)
    parts = lax.all_to_all(projected.reshape(passages * layers, owned, width), ("passage", "span"), 0, 0, tiled=True)
    basis, inv = basis_of(inner, rim, last, gram, math.sqrt(row_total))
    coefficients = coefficients_of(parts, inv, 1.0 / math.sqrt(row_total))
    return basis.reshape(3 * variables, cells, lines, width), coefficients


def solution(mesh):
    return jax.shard_map(
        shards,
        mesh=mesh,
        in_specs=(P(None, "passage", "span", None), P(), P("passage"), P(), P("span")),
        out_specs=(P(None, "passage", "span", None), P(("passage", "span"), None)),
        check_vma=False,
    )
```

```python
import functools
import math

import jax
import jax.numpy as jnp
from jax import lax
from jax.experimental import pallas as pl
from jax.experimental.pallas import tpu as pltpu
from jax.sharding import PartitionSpec as P

F32 = jnp.float32
BF16 = jnp.bfloat16
MIB = 1024 * 1024
K1_MIB = 24
K1_CHUNKS = 4
K4_BLOCKS = 5
K2_MIB = 24
K3_MIB = 24
K4_MIB = 24


def in_hbm(x):
    return pltpu.with_memory_space_constraint(x, pltpu.HBM)


def params(mib, **kw):
    return pltpu.CompilerParams(vmem_limit_bytes=mib * MIB, **kw)


def packed_rows(rows, groups):
    return rows + rows // groups


def pack(dst_ref, v, value, groups):
    rows, width = value.shape
    part = rows // groups
    rest = value[:, 128:]
    tail = [rest[g * part:(g + 1) * part] for g in range(groups)]
    spare = 128 - groups * (width - 128)
    if spare:
        tail.append(jnp.zeros((part, spare), value.dtype))
    dst_ref[v, :rows] = value[:, :128].astype(BF16)
    dst_ref[v, rows:] = jnp.concatenate(tail, axis=1).astype(BF16)


def unpack(dst_ref, src_ref, v, groups):
    rows, width = dst_ref.shape
    part = rows // groups
    extra = width - 128
    dst_ref[:, :128] = src_ref[v, :rows].astype(F32)
    rest = src_ref[v, rows:].astype(F32)
    for g in range(groups):
        dst_ref[g * part:(g + 1) * part, 128:] = rest[:, g * extra:(g + 1) * extra]


T_GROUPS = 6
R_GROUPS = 4
VMEM_SPEC = pl.BlockSpec(memory_space=pltpu.VMEM)
HBM_SPEC = pl.BlockSpec(memory_space=pltpu.HBM)


def fields_kernel(radial_total, lines, blade_hbm, speed_hbm, sketch_hbm, snap_hbm,
                  field_ref, y_ref, first_t_ref, last_t_ref, first_r_ref, last_r_ref,
                  blade_ref, speed_ref, sketch_ref, turned_ref, low_r_ref, high_r_ref, small_sems, sems):
    variables, rows, columns = field_ref.shape
    chunks = sems.shape[0]
    part = rows // chunks
    group = 2 * lines
    cells = part // lines
    spare = rows // lines
    small = [pltpu.make_async_copy(blade_hbm, blade_ref, small_sems.at[0]),
             pltpu.make_async_copy(speed_hbm, speed_ref, small_sems.at[1]),
             pltpu.make_async_copy(sketch_hbm, sketch_ref, small_sems.at[2])]
    for copy in small:
        copy.start()

    def copy_of(c):
        at = pl.ds(pl.multiple_of(c * part, part), part)
        return pltpu.make_async_copy(snap_hbm.at[:, at], field_ref.at[:, at], sems.at[c])

    for c in range(chunks):
        copy_of(c).start()
    row_id = lax.broadcasted_iota(jnp.int32, (group, 128), 0)
    line_id = jnp.where(row_id >= lines, row_id - lines, row_id)
    radial_pos = (lax.axis_index("span") * lines + line_id).astype(F32)
    radius = 0.6 + 0.4 * (radial_pos + 0.5) / radial_total
    for copy in small:
        copy.wait()
    turned_ref[...] = sketch_ref[...].T

    def column_speed(cell):
        label = blade_ref[cell]
        total = jnp.float32(0.0)
        for row in range(speed_ref.shape[0]):
            total = jnp.where(label == row, speed_ref[row], total)
        return total

    def one_chunk(c, carry):
        copy_of(c).wait()
        base = pl.multiple_of(c * part, part)
        def one_pair(pair, carry):
            cell = c * cells + 2 * pair
            speed = jnp.where(row_id < lines, column_speed(cell), column_speed(cell + 1))
            shift = speed * radius
            at = pl.ds(pl.multiple_of(base + pair * group, group), group)
            for tile in range(columns // 128):
                lanes = pl.ds(tile * 128, 128)
                density = field_ref[0, at, lanes].astype(F32)
                axial = field_ref[1, at, lanes].astype(F32)
                swirl = field_ref[2, at, lanes].astype(F32) + shift
                radial = field_ref[3, at, lanes].astype(F32)
                kinetic = axial * axial + swirl * swirl + radial * radial
                press = (field_ref[4, at, lanes].astype(F32)
                         + 0.05 * (1.0 + 0.2 * jnp.tanh(density)) * kinetic)
                field_ref[2, at, lanes] = swirl.astype(BF16)
                field_ref[4, at, lanes] = press.astype(BF16)
            return carry

        lax.fori_loop(0, part // group, one_pair, 0)
        block = pl.ds(base, part)
        y = jnp.dot(field_ref[:, block].reshape(variables * part, columns), turned_ref[...],
                    preferred_element_type=F32)
        for v in range(variables):
            y_ref[v, block] = y[v * part:(v + 1) * part]
            for cell in range(cells):
                for side in range(2):
                    to = pl.ds(side * spare + c * cells + cell, 1)
                    row = v * part + cell * lines + side
                    low_r_ref[v, to] = y[row:row + 1]
                    row = row + lines - 2
                    high_r_ref[v, to] = y[row:row + 1]
        return carry

    lax.fori_loop(0, chunks, one_chunk, 0)
    for v in range(variables):
        pack(first_t_ref, v, y_ref[v, :4 * lines], T_GROUPS)
        pack(last_t_ref, v, y_ref[v, rows - 4 * lines:], T_GROUPS)
        pack(first_r_ref, v, low_r_ref[v], R_GROUPS)
        pack(last_r_ref, v, high_r_ref[v], R_GROUPS)


def fields_and_sketch(snapshots, sketch_t, blade_row, row_speed, lines, radial_total):
    variables, rows, columns = snapshots.shape
    width = sketch_t.shape[0]
    chunks = K1_CHUNKS
    cells = rows // lines
    edge_t = jax.ShapeDtypeStruct((variables, packed_rows(4 * lines, T_GROUPS), 128), BF16)
    edge_r = jax.ShapeDtypeStruct((variables, packed_rows(2 * cells, R_GROUPS), 128), BF16)
    return pl.pallas_call(
        functools.partial(fields_kernel, radial_total, lines),
        in_specs=[HBM_SPEC] * 4,
        out_specs=[VMEM_SPEC] * 6,
        out_shape=[
            jax.ShapeDtypeStruct((variables, rows, columns), BF16),
            jax.ShapeDtypeStruct((variables, rows, width), F32),
            edge_t, edge_t, edge_r, edge_r,
        ],
        scratch_shapes=[
            pltpu.SMEM(blade_row.shape, blade_row.dtype),
            pltpu.SMEM(row_speed.shape, row_speed.dtype),
            pltpu.VMEM(sketch_t.shape, sketch_t.dtype),
            pltpu.VMEM(sketch_t.shape[::-1], sketch_t.dtype),
            pltpu.VMEM((variables, 2 * cells, width), F32),
            pltpu.VMEM((variables, 2 * cells, width), F32),
            pltpu.SemaphoreType.DMA((3,)),
            pltpu.SemaphoreType.DMA((chunks,)),
        ],
        compiler_params=params(K1_MIB),
        name="fields_sketch",
    )(in_hbm(blade_row), in_hbm(row_speed), in_hbm(sketch_t), in_hbm(snapshots))


def rounded(x):
    return x.astype(BF16).astype(F32)


def shift_down(x, end):
    return jnp.where(lax.broadcasted_iota(jnp.int32, x.shape, 0) == 0, end, pltpu.roll(x, 1, 0))


def shift_up(x, end):
    last = x.shape[0] - 1
    return jnp.where(lax.broadcasted_iota(jnp.int32, x.shape, 0) == last, end, pltpu.roll(x, last, 0))


def turn(wide, scale, get, t):
    return scale * jnp.where(wide, get(t + 2) - get(t - 2), get(t + 1) - get(t - 1))


def inner_kernel(lines, reach_ref, y_ref, z_out, z_ref, gram_ref, sems):
    variables, rows, width = y_ref.shape
    cells = rows // lines
    wide = reach_ref[...] == 2
    scale = jnp.where(wide, 0.25, 0.5)
    inner = pl.ds(2 * lines, rows - 4 * lines)

    def copies_of(v):
        return [pltpu.make_async_copy(z_ref.at[0, v], z_out.at[0, v], sems.at[0, v]),
                pltpu.make_async_copy(z_ref.at[1, v, inner], z_out.at[1, v, inner], sems.at[1, v])]

    gram_ref[...] = jnp.zeros_like(gram_ref)

    def one_variable(v, carry):
        def y_at(t):
            return y_ref[v, t * lines:(t + 1) * lines, :]

        for pair in range(cells // 2):
            at = pl.ds(2 * pair * lines, 2 * lines)
            z_ref[0, v, at, :] = y_ref[v, at, :].astype(BF16)
            if 0 < pair < cells // 2 - 1:
                z1 = [turn(wide, scale, y_at, t) for t in (2 * pair, 2 * pair + 1)]
                z_ref[1, v, at, :] = jnp.concatenate(z1, axis=0).astype(BF16)
        for copy in copies_of(v):
            copy.start()
        for z in (z_ref[0, v], z_ref[1, v, inner]):
            gram_ref[...] += lax.dot_general(z, z, (((0,), (0,)), ((), ())), preferred_element_type=F32)
        return carry

    lax.fori_loop(0, variables, one_variable, 0)
    for v in range(variables):
        for copy in copies_of(v):
            copy.wait()


def inner_stencils(y, reach, lines):
    variables, rows, width = y.shape
    return pl.pallas_call(
        functools.partial(inner_kernel, lines),
        in_specs=[VMEM_SPEC] * 2,
        out_specs=[HBM_SPEC, VMEM_SPEC, VMEM_SPEC],
        out_shape=[
            pltpu.HBM((2, variables, rows, width), BF16),
            jax.ShapeDtypeStruct((2, variables, rows, width), BF16),
            jax.ShapeDtypeStruct((width, width), F32),
        ],
        scratch_shapes=[pltpu.SemaphoreType.DMA((2, variables))],
        compiler_params=params(16),
        cost_estimate=pl.CostEstimate(flops=4 * variables * rows * 256 * 256, bytes_accessed=variables * rows * 2048,
                                      transcendentals=0),
        name="inner_stencils",
    )(reach, y)


def outer_kernel(lines, reach_ref, y_ref, before_t_in, after_t_in, before_r_in, after_r_in, inner_gram_ref,
                 rim_out, z_out, z_ref, edge_t_ref, edge_r_ref, gram_ref,
                 acc_ref, before_t_ref, after_t_ref, before_r_ref, after_r_ref, rim_ref, sems):
    variables, rows, width = y_ref.shape
    cells = rows // lines
    wide = reach_ref[...] == 2
    scale = jnp.where(wide, 0.25, 0.5)
    span = lax.axis_index("span")
    has_before = jnp.where(span > 0, 0.5, 0.0).astype(F32)
    has_after = jnp.where(span < lax.axis_size("span") - 1, 0.5, 0.0).astype(F32)

    def copies_of(v):
        return [pltpu.make_async_copy(rim_ref.at[v], rim_out.at[v], sems.at[0, v]),
                pltpu.make_async_copy(z_ref.at[v], z_out.at[v], sems.at[1, v])]

    acc_ref[...] = inner_gram_ref[...]

    def one_variable(v, carry):
        unpack(before_t_ref, before_t_in, v, T_GROUPS)
        unpack(after_t_ref, after_t_in, v, T_GROUPS)
        unpack(before_r_ref, before_r_in, v, R_GROUPS)
        unpack(after_r_ref, after_r_in, v, R_GROUPS)

        def y_at(t):
            if t < 0:
                return before_t_ref[(t + 4) * lines:(t + 5) * lines, :]
            if t >= cells:
                return after_t_ref[(t - cells) * lines:(t - cells + 1) * lines, :]
            return y_ref[v, t * lines:(t + 1) * lines, :]

        rim = [turn(wide, scale, y_at, t) for t in RIM_FIRST + tuple(cells + t for t in RIM_LAST)]
        for k, slab in enumerate(rim):
            edge_t_ref[v, k] = rounded(slab)
        rim_ref[v] = jnp.concatenate(rim[2:6], axis=0).astype(BF16)
        for pair in range(cells // 2):
            kept = []
            for t in (2 * pair, 2 * pair + 1):
                y = y_at(t)
                one, two = slice(t, t + 1), slice(cells + t, cells + t + 1)
                edge_r_ref[v, one, :] = rounded(has_before * (y[0:1] - before_r_ref[one, :]))
                edge_r_ref[v, two, :] = rounded(has_after * (after_r_ref[two, :] - y[lines - 1:lines]))
                kept.append(0.5 * (shift_up(y, after_r_ref[one, :]) - shift_down(y, before_r_ref[two, :])))
            z_ref[v, pl.ds(2 * pair * lines, 2 * lines), :] = jnp.concatenate(kept, axis=0).astype(BF16)
        for copy in copies_of(v):
            copy.start()
        for z in (rim_ref[v], z_ref[v]):
            acc_ref[...] += lax.dot_general(z, z, (((0,), (0,)), ((), ())), preferred_element_type=F32)
        return carry

    lax.fori_loop(0, variables, one_variable, 0)
    gram_ref[:width, :] = acc_ref[:, :128]
    gram_ref[width:, :] = jnp.zeros((gram_ref.shape[0] - width, 128), F32)
    gram_ref[width:, :width - 128] = acc_ref[128:, 128:]
    for v in range(variables):
        for copy in copies_of(v):
            copy.wait()


RIM_FIRST = (-2, -1, 0, 1)
RIM_LAST = (-2, -1, 0, 1)


def outer_stencils(y, before_t, after_t, before_r, after_r, inner_gram, reach, lines):
    variables, rows, width = y.shape
    cells = rows // lines
    return pl.pallas_call(
        functools.partial(outer_kernel, lines),
        in_specs=[VMEM_SPEC] * 7,
        out_specs=[HBM_SPEC] * 2 + [VMEM_SPEC] * 4,
        out_shape=[
            pltpu.HBM((variables, 4 * lines, width), BF16),
            pltpu.HBM((variables, rows, width), BF16),
            jax.ShapeDtypeStruct((variables, rows, width), BF16),
            jax.ShapeDtypeStruct((variables, 8, lines, width), F32),
            jax.ShapeDtypeStruct((variables, 2 * cells, width), F32),
            jax.ShapeDtypeStruct((width + (width - 128), 128), F32),
        ],
        scratch_shapes=[
            pltpu.VMEM((width, width), F32),
            pltpu.VMEM((4 * lines, width), F32),
            pltpu.VMEM((4 * lines, width), F32),
            pltpu.VMEM((2 * cells, width), F32),
            pltpu.VMEM((2 * cells, width), F32),
            pltpu.VMEM((variables, 4 * lines, width), BF16),
            pltpu.SemaphoreType.DMA((2, variables)),
        ],
        compiler_params=params(K2_MIB),
        name="outer_stencils",
    )(reach, y, before_t, after_t, before_r, after_r, inner_gram)


def transposed_kernel(lines, reach_ref, z_ref, z2_ref, edge_t_ref, edge_r_ref, w_ref):
    _, variables, rows, width = z_ref.shape
    cells = rows // lines
    wide = reach_ref[...] == 2
    scale = jnp.where(wide, 0.25, 0.5)

    def one_variable(v, carry):
        slabs = {}

        def z1_at(t):
            if t < 2:
                return edge_t_ref[v, t + 2]
            if t >= cells - 2:
                return edge_t_ref[v, t - cells + 6]
            if t not in slabs:
                first = t - t % 2
                both = z_ref[1, v, first * lines:(first + 2) * lines, :].astype(F32)
                slabs[first], slabs[first + 1] = both[:lines], both[lines:]
            return slabs[t]

        for pair in range(cells // 2):
            at = slice(2 * pair * lines, 2 * (pair + 1) * lines)
            z0 = z_ref[0, v, at, :].astype(F32)
            z2 = z2_ref[v, at, :].astype(F32)
            out = []
            for k in range(2):
                t = 2 * pair + k
                part = slice(k * lines, (k + 1) * lines)
                w2 = (shift_down(z2[part], edge_r_ref[v, t:t + 1, :])
                      - shift_up(z2[part], edge_r_ref[v, cells + t:cells + t + 1, :]))
                out.append(z0[part] - turn(wide, scale, z1_at, t) + 0.5 * w2)
            w_ref[v, at, :] = jnp.concatenate(out, axis=0).astype(BF16)
        return carry

    lax.fori_loop(0, variables, one_variable, 0)


def transposed_stencils(z, z2, edge_t, edge_r, reach, lines):
    _, variables, rows, width = z.shape
    return pl.pallas_call(
        functools.partial(transposed_kernel, lines),
        in_specs=[VMEM_SPEC] * 5,
        out_specs=VMEM_SPEC,
        out_shape=jax.ShapeDtypeStruct((variables, rows, width), BF16),
        compiler_params=params(16),
        name="transposed_stencils",
    )(reach, z, z2, edge_t, edge_r)


def project_kernel(field_ref, w_ref, out_ref, acc_ref):
    for v in range(field_ref.shape[0]):
        part = lax.dot_general(w_ref[v], field_ref[v], (((0,), (0,)), ((), ())), preferred_element_type=F32)
        acc_ref[...] = part if v == 0 else acc_ref[...] + part
    out_ref[...] = acc_ref[...].T.astype(BF16)


def project(fields, w):
    variables, rows, columns = fields.shape
    width = w.shape[2]
    return pl.pallas_call(
        project_kernel,
        in_specs=[VMEM_SPEC] * 2,
        out_specs=VMEM_SPEC,
        out_shape=jax.ShapeDtypeStruct((columns, width), BF16),
        scratch_shapes=[pltpu.VMEM((width, columns), F32)],
        compiler_params=params(K3_MIB),
        cost_estimate=pl.CostEstimate(flops=2 * variables * rows * columns * 256,
                                      bytes_accessed=variables * rows * columns * 2, transcendentals=0),
        name="project",
    )(fields, w)


def split3(x):
    high = x.astype(BF16)
    rest = x - high.astype(F32)
    mid = rest.astype(BF16)
    return high, mid, (rest - mid.astype(F32)).astype(BF16)


def inverse_factor_of(width, gram_ref, out_ref, a_ref):
    size = 16
    packed = gram_ref[...]
    a_ref[...] = jnp.zeros_like(a_ref)
    a_ref[:, :128] = packed[:width]
    a_ref[:128, 128:width] = packed[128:width].T
    a_ref[128:, 128:width] = packed[width:, :width - 128]
    a_ref[:, 256:] = jnp.where(
        lax.broadcasted_iota(jnp.int32, (width, 256), 0) == lax.broadcasted_iota(jnp.int32, (width, 256), 1),
        1.0, 0.0)
    row = lax.broadcasted_iota(jnp.int32, (size, 128), 0)
    lane = lax.broadcasted_iota(jnp.int32, (size, 256), 1)
    for start in range(0, width, size):
        panels = [a_ref[start:start + size, tile * 128:(tile + 1) * 128] for tile in range(4)]
        tile, offset = start // 128, start % 128
        cols = [jnp.broadcast_to(panels[tile][:, offset + j:offset + j + 1], (size, 128)) for j in range(size)]
        for j in range(size):
            pivot = jnp.broadcast_to(cols[j][j:j + 1, :], (size, 128))
            inv = lax.rsqrt(pivot)
            inv = inv * (1.5 - 0.5 * pivot * inv * inv)
            low = cols[j] * inv
            for i in range(j + 1, size):
                cols[i] = cols[i] - low * jnp.broadcast_to(low[i:i + 1, :], (size, 128))
            below = jnp.where(row > j, low, 0.0)
            for p in range(4):
                lead = jnp.broadcast_to(panels[p][j:j + 1, :], (size, 128)) * inv
                panels[p] = jnp.where(row == j, lead, panels[p] - below * lead)
        out_ref[start:start + size, :] = jnp.concatenate([panels[2], panels[3]], axis=1)[:, :width]
        if start + size < width:
            whole = jnp.concatenate(panels, axis=1)
            left = jnp.where(lane >= start + size, whole[:, :256], 0.0)
            lh, lm, ll = split3(left)
            rh, rm, rl = split3(whole)
            lhs = jnp.concatenate([lh, lh, lm, lm, lh, ll], axis=0)
            rhs = jnp.concatenate([rh, rm, rh, rm, rl, rh], axis=0)
            update = lax.dot_general(lhs, rhs, (((0,), (0,)), ((), ())), preferred_element_type=F32)
            a_ref[start + size:, :] -= update[start + size:width, :]


def basis_kernel(scale, gram_ref, inner_hbm, rim_hbm, last_hbm, out_hbm, inv_ref, a_ref, high_ref, low_ref,
                 z_ref, out_ref, z_sems, sems):
    width = z_ref.shape[2]
    blocks = sems.shape[0]
    group = z_ref.shape[0] // blocks
    rows = group * z_ref.shape[1]
    variables, rim = rim_hbm.shape[:2]
    cells = last_hbm.shape[1]
    half = rim // 2
    middle = pl.ds(half, cells - rim)
    second = z_ref.at[pl.ds(variables, variables)]
    pieces = [
        (inner_hbm.at[0], z_ref.at[pl.ds(0, variables)]),
        (inner_hbm.at[1, :, middle], second.at[:, middle]),
        (rim_hbm.at[:, pl.ds(0, half)], second.at[:, pl.ds(0, half)]),
        (rim_hbm.at[:, pl.ds(half, half)], second.at[:, pl.ds(cells - half, half)]),
        (last_hbm, z_ref.at[pl.ds(2 * variables, variables)]),
    ]
    z_copies = [pltpu.make_async_copy(source, target, z_sems.at[k]) for k, (source, target) in enumerate(pieces)]
    for copy in z_copies:
        copy.start()
    inverse_factor_of(width, gram_ref, inv_ref, a_ref)
    turned = inv_ref[...].T * scale
    high_ref[...] = turned.astype(BF16)
    low_ref[...] = (turned - high_ref[...].astype(F32)).astype(BF16)
    for copy in z_copies:
        copy.wait()

    def copy_of(i):
        at = pl.ds(pl.multiple_of(i * rows, rows), rows)
        return pltpu.make_async_copy(out_ref.at[at], out_hbm.at[at], sems.at[i])

    def one_block(i, carry):
        at = pl.ds(pl.multiple_of(i * rows, rows), rows)
        z = z_ref[pl.ds(i * group, group)].reshape(rows, width)
        out_ref[at] = (jnp.dot(z, low_ref[...], preferred_element_type=F32)
                       + jnp.dot(z, high_ref[...], preferred_element_type=F32))
        copy_of(i).start()
        return carry

    lax.fori_loop(0, blocks, one_block, 0)
    for i in range(blocks):
        copy_of(i).wait()


def basis_of(inner, rim, last, gram, scale):
    variables, cells, width = last.shape
    rows = 3 * variables * cells
    return pl.pallas_call(
        functools.partial(basis_kernel, scale),
        in_specs=[VMEM_SPEC] + [HBM_SPEC] * 3,
        out_specs=[HBM_SPEC, VMEM_SPEC],
        out_shape=[pltpu.HBM((rows, width), F32), jax.ShapeDtypeStruct((width, width), F32)],
        scratch_shapes=[pltpu.VMEM((width, 512), F32), pltpu.VMEM((width, width), BF16),
                        pltpu.VMEM((width, width), BF16), pltpu.VMEM((3 * variables, cells, width), BF16),
                        pltpu.VMEM((rows, width), F32), pltpu.SemaphoreType.DMA((5,)),
                        pltpu.SemaphoreType.DMA((K4_BLOCKS,))],
        compiler_params=params(K4_MIB),
        cost_estimate=pl.CostEstimate(flops=1000, bytes_accessed=1000, transcendentals=0),
        name="basis",
    )(gram, in_hbm(inner), in_hbm(rim), in_hbm(last))


def coefficients_kernel(scale, parts_ref, inv_ref, out_ref):
    owned = jnp.sum(parts_ref[...].astype(F32), axis=0)
    out_ref[...] = lax.dot_general(owned, inv_ref[...], (((1,), (1,)), ((), ())),
                                   precision=lax.Precision.HIGHEST, preferred_element_type=F32) * scale


def coefficients_of(parts, inv, scale):
    _, rows, width = parts.shape
    return pl.pallas_call(
        functools.partial(coefficients_kernel, scale),
        in_specs=[pl.BlockSpec(memory_space=pltpu.VMEM)] * 2,
        out_specs=pl.BlockSpec(memory_space=pltpu.VMEM),
        out_shape=jax.ShapeDtypeStruct((rows, width), F32),
        compiler_params=params(32),
        name="coefficients",
    )(parts, inv)


def reduce_all(x, start, finish):
    passages, layers = lax.axis_size("passage"), lax.axis_size("span")

    def exchange(x, axis, length, moves, meanwhile=None):
        parts = [lax.ppermute(x, axis, [(i, move(i)) for i in range(length)]) for move in moves]
        if meanwhile is not None:
            parts, meanwhile = lax.optimization_barrier((parts, meanwhile))
        for part in parts:
            x = x + part
        return x, meanwhile

    w = start()
    x, w = exchange(x, "passage", passages, [lambda i, k=k: (i + 2 * k) % passages for k in (1, 3, 2)], w)
    projected = finish(w)
    x, projected = exchange(x, "span", layers, [lambda i, k=k: i // 4 * 4 + (i + k) % 4 for k in (1, 3, 2)],
                            projected)
    x, _ = exchange(x, "span", layers, [lambda i, k=k: (i + 4 * k) % layers for k in (1, 3, 2)])
    x, _ = exchange(x, "passage", passages, [lambda i: i ^ 1])
    return x, projected


def shards(snapshots, sketch, blade_row, row_speed, stencil_reach):
    variables, cells, lines, columns = snapshots.shape
    width = sketch.shape[1]
    passages, layers = lax.axis_size("passage"), lax.axis_size("span")
    row_total = 3 * variables * cells * passages * lines * layers
    fields, y, first_t, last_t, first_r, last_r = fields_and_sketch(
        snapshots.reshape(variables, cells * lines, columns), sketch.T, blade_row, row_speed,
        lines, lines * layers)
    ring_up = [(i, (i + 1) % passages) for i in range(passages)]
    ring_down = [(j, i) for i, j in ring_up]
    line_up = [(i, i + 1) for i in range(layers - 1)]
    line_down = [(j, i) for i, j in line_up]
    before_r = lax.ppermute(last_r, "span", line_up)
    after_r = lax.ppermute(first_r, "span", line_down)
    before_t = lax.ppermute(last_t, "passage", ring_up)
    after_t = lax.ppermute(first_t, "passage", ring_down)
    reach = jnp.broadcast_to(stencil_reach[:, None], (lines, width))
    inner, held, inner_gram = inner_stencils(y, reach, lines)
    halos, inner_gram = lax.optimization_barrier(((before_t, after_t, before_r, after_r), inner_gram))
    rim, last, z2, edge_t, edge_r, gram = outer_stencils(y, *halos, inner_gram, reach, lines)
    gram, projected = reduce_all(
        gram, lambda: transposed_stencils(held, z2, edge_t, edge_r, reach, lines), lambda w: project(fields, w))
    owned = columns // (passages * layers)
    parts = lax.all_to_all(projected.reshape(passages * layers, owned, width), ("passage", "span"), 0, 0, tiled=True)
    basis, inv = basis_of(inner, rim, last, gram, math.sqrt(row_total))
    coefficients = coefficients_of(parts, inv, 1.0 / math.sqrt(row_total))
    return basis.reshape(3 * variables, cells, lines, width), coefficients


def solution(mesh):
    return jax.shard_map(
        shards,
        mesh=mesh,
        in_specs=(P(None, "passage", "span", None), P(), P("passage"), P(), P("span")),
        out_specs=(P(None, "passage", "span", None), P(("passage", "span"), None)),
        check_vma=False,
    )
```
